128 devices in a mesh: src: 4 (over y), seq: 32 (over x, z, core).
Axes of the slice: x: 4, y: 4, z: 4, core: 2. Of those that a mesh axis runs over, the one named last changes fastest.
Arguments:
- kv_delta: bfloat16 [16, 32, 32, 16, 2048], P('src', None, 'seq'), may hold values from -6 to 6
- anchors: bfloat16 [16, 32, 32, 2048], P('src', None, 'seq'), may hold values from -6 to 6
- scales: float32 [16, 32, 32, 16], P('src', None, 'seq'), may hold values from 0.1 to 1
- in_len: int32 [16], replicated, may hold values from 1 to 16384, 131072 in all
- assign: int32 [16], replicated, may hold values from 0 to 15, as said below
- res_cache: bfloat16 [16, 8192, 2048], P('src', 'seq'), may hold values from -6 to 6
- res_len: int32 [16], replicated, may hold values from 1 to 8192, 65536 in all
- queries: bfloat16 [32, 4, 8192], P('src'), may hold values from -110 to 110
- fresh_key_value: bfloat16 [32, 4, 2048], P('src'), may hold values from -6 to 6
Outputs:
- in_cache: bfloat16 [16, 16384, 2048], P('src', 'seq')
- attention: bfloat16 [32, 4, 8192], P('src')
The draws below stay inside these ranges and needn't reach their ends.
Inputs may be any that keep to these rules, and one draw needn't show every extreme that they name: `assign`: a permutation of the incoming slots; decode replica p holds slots p * 4 to (p + 1) * 4 - 1 and receives exactly 1 request from each prefill replica.
All inputs are finite; a program needn't handle non-finite values.
Results may differ from the reference program's by a relative error of at most 0.012.
The reference program's roundings to bfloat16 on the way count: a program that leaves them out, or rounds other values in their place, can miss the bound.
Values may be sent and summed in bfloat16 or wider, within the bound.
A program may use at most 192 MiB of HBM per device.

```python
import math
import jax
import jax.numpy as jnp
import numpy as np
from jax import lax

QUERY_HEADS = 64
KEY_VALUE_HEADS = 8
HEAD_SIZE = 128
GRP = 16
DECODE_STEPS = 4
PAIR = 1
RR = 4
REPLICA_REQUESTS = 4
DECODE_SLOTS = 8
INCOMING_TOTAL = 16
RESIDENT_TOTAL = 16
CACHE_POSITIONS = 16384
RES_CAP = 8192
FEAT = 2048
N_SRC = 4
N_SEQ = 32


def draw_assign(key, part):
    key = jax.random.fold_in(key, 11)
    rank_key, seat_key = jax.random.split(key)
    ranks = jnp.stack([jax.random.permutation(jax.random.fold_in(rank_key, source_index), REPLICA_REQUESTS) for source_index in range(N_SRC)])
    seats = jnp.stack([jax.random.permutation(jax.random.fold_in(seat_key, replica_index), REPLICA_REQUESTS) for replica_index in range(N_SRC)])
    target = ranks // PAIR
    within = ranks % PAIR
    sources = jnp.arange(N_SRC)[:, None]
    local_seat = seats[target, sources * PAIR + within]
    return (target * REPLICA_REQUESTS + local_seat).reshape(INCOMING_TOTAL).astype(jnp.int32)


def draw_queries(key, part):
    key = jax.random.fold_in(key, 23)
    noise_key = jax.random.fold_in(key, 0)
    shape_full = (N_SRC * DECODE_SLOTS, DECODE_STEPS, QUERY_HEADS, HEAD_SIZE)
    values = jnp.clip(jax.random.normal(noise_key, shape_full, jnp.float32), -6.0, 6.0)
    return values.reshape(N_SRC * DECODE_SLOTS, DECODE_STEPS, QUERY_HEADS * HEAD_SIZE).astype(jnp.bfloat16)


def steps_of(rng, dims, cuts, low, top_value):
    def one(dim, blocks):
        draws = jax.random.uniform(jax.random.fold_in(jax.random.fold_in(rng, 6), dim), (blocks,), jnp.float32, low / len(cuts), top_value / len(cuts))
        return jnp.repeat(jnp.exp(draws), dims[dim] // blocks).reshape((-1,) + (1,) * (len(dims) - dim - 1))

    loudness = one(*cuts[0])
    for cut in cuts[1:]:
        loudness = loudness * one(*cut)
    return loudness


def profile(number_of, total, limit, lean):
    loads = [(1 << 20) // math.isqrt(rank ** lean) + 1 for rank in range(2, number_of + 1)]
    spare, given = total - limit - (number_of - 1), [1] * (number_of - 1)
    while spare > 0:
        movable = [i for i in range(number_of - 1) if given[i] < limit]
        mass, left = sum([loads[i] for i in movable]), spare
        for i in movable:
            extra = min(limit - given[i], max(1, left * loads[i] // mass), spare)
            given[i] = given[i] + extra
            spare = spare - extra
    return np.array([limit] + given)


def uneven_parts(key, count, total, reach, lean):
    if count == 2:
        one = jax.random.randint(key, (), max(1, total - reach), min(reach, total - 1) + 1)
        return jnp.stack([one, total - one])
    sizes = jnp.asarray(profile(count, total, reach, lean), jnp.int32)
    couples = (count - 1) // 2
    donor, taker = sizes[1:1 + 2 * couples:2], sizes[2:2 + 2 * couples:2]
    slack = jnp.minimum(donor - 1, reach - taker)
    moved = jax.random.randint(jax.random.fold_in(key, 1), (couples,), 0, 1 << 20) % (slack + 1)
    sizes = sizes.at[1:1 + 2 * couples:2].set(donor - moved).at[2:2 + 2 * couples:2].set(taker + moved)
    return sizes[jax.random.permutation(jax.random.fold_in(key, 2), count)]


def normal_values(own_key, shape, scale, limit, shards=(), held_as=jnp.bfloat16):
    loudness = steps_of(own_key, shape, shards, -0.22, 0.18) if shards else 1.0
    values = jax.random.normal(own_key, shape, jnp.float32) * scale * loudness
    return jnp.minimum(jnp.maximum(values, -limit), limit).astype(held_as)


def setup_inputs(seed: int = 0) -> dict:
    key_list = jax.random.split(jax.random.key(seed), 10)
    return {
        "kv_delta": normal_values(key_list[0], (INCOMING_TOTAL, N_SEQ, N_SEQ, GRP, FEAT), 1.0, 6.0, ((0, 4), (2, 32))),
        "anchors": normal_values(key_list[1], (INCOMING_TOTAL, N_SEQ, N_SEQ, FEAT), 1.0, 6.0, ((0, 4), (2, 32))),
        "scales": jnp.clip(jnp.exp(math.log(1.0) - 2.3025851 * jax.random.uniform(key_list[2], (INCOMING_TOTAL, N_SEQ, N_SEQ, 2 * KEY_VALUE_HEADS), jnp.float32) ** steps_of(key_list[2], (INCOMING_TOTAL, N_SEQ, N_SEQ, 2 * KEY_VALUE_HEADS), ((0, 4), (2, 32)), -0.2, 0.2)), 0.1, 1.0),
        "in_len": uneven_parts(key_list[3], INCOMING_TOTAL, INCOMING_TOTAL * CACHE_POSITIONS // 2, CACHE_POSITIONS, 2).astype(jnp.int32),
        "assign": draw_assign(jax.random.fold_in(key_list[9], 71), 0),
        "res_cache": normal_values(key_list[5], (RESIDENT_TOTAL, RES_CAP, FEAT), 1.0, 6.0, ((0, 4), (1, 32))),
        "res_len": uneven_parts(key_list[6], RESIDENT_TOTAL, RESIDENT_TOTAL * RES_CAP // 2, RES_CAP, 2).astype(jnp.int32),
        "queries": draw_queries(jax.random.fold_in(key_list[9], 71), 0),
        "fresh_key_value": normal_values(key_list[8], (N_SRC * DECODE_SLOTS, DECODE_STEPS, FEAT), 1.0, 6.0, ((0, 4),)),
    }


def rebuild_one(delta_one, anchor_one, scale_one):
    scale_wide = jnp.repeat(scale_one, HEAD_SIZE, axis=-1)
    restored_cache = anchor_one.astype(jnp.float32)[:, :, None, :] + scale_wide[:, :, None, :] * delta_one.astype(jnp.float32)
    return restored_cache.astype(jnp.bfloat16).reshape(CACHE_POSITIONS, 2 * KEY_VALUE_HEADS * HEAD_SIZE)

def attend_one(single_query_row, cached_row_list, cache_len, new_rows):
    key_span_width = KEY_VALUE_HEADS * HEAD_SIZE
    query_head_list = single_query_row.astype(jnp.float32).reshape(DECODE_STEPS, KEY_VALUE_HEADS, QUERY_HEADS // KEY_VALUE_HEADS, HEAD_SIZE)
    every_row = jnp.concatenate([cached_row_list, new_rows], axis=0).astype(jnp.float32)
    key_row_list = every_row[:, :key_span_width].reshape(-1, KEY_VALUE_HEADS, HEAD_SIZE)
    value_row_list = every_row[:, key_span_width:].reshape(-1, KEY_VALUE_HEADS, HEAD_SIZE)
    scores = jnp.einsum('shgd,thd->hsgt', query_head_list, key_row_list) / math.sqrt(HEAD_SIZE)
    span_len = cached_row_list.shape[0]
    cache_ok = jnp.arange(span_len) < cache_len
    new_ok = jnp.arange(DECODE_STEPS)[None, :] <= jnp.arange(DECODE_STEPS)[:, None]
    keep_mask = jnp.concatenate([jnp.broadcast_to(cache_ok[None, :], (DECODE_STEPS, span_len)), new_ok], axis=1)
    keep_mask = keep_mask[None, :, None, :]
    scores = jnp.where(keep_mask, scores, -1e+30)
    row_peak = lax.optimization_barrier(jnp.max(scores, axis=-1, keepdims=True))
    weights = jnp.where(keep_mask, jnp.exp(scores - row_peak), 0.0)
    row_total = lax.optimization_barrier(jnp.sum(weights, axis=-1, keepdims=True))
    rounded = lax.optimization_barrier(weights.astype(jnp.bfloat16)).astype(jnp.float32)
    summed = jnp.einsum('hsgt,thd->hsgd', rounded, value_row_list)
    result = summed / row_total
    return result.transpose(1, 0, 2, 3).reshape(DECODE_STEPS, QUERY_HEADS * HEAD_SIZE).astype(jnp.bfloat16)

def reference(kv_delta, anchors, scales, in_len, assign, res_cache, res_len, queries, fresh_key_value):
    holder = jnp.argsort(assign).astype(jnp.int32)

    def rebuild_slot(request):
        full_rows = rebuild_one(kv_delta[request], anchors[request], scales[request])
        live_rows = jnp.arange(CACHE_POSITIONS) < in_len[request]
        return jnp.where(live_rows[:, None], full_rows, jnp.zeros_like(full_rows))
    in_cache = lax.map(rebuild_slot, holder)
    slot_len = in_len[holder]
    query_grid = queries.reshape(N_SRC, DECODE_SLOTS, DECODE_STEPS, QUERY_HEADS * HEAD_SIZE)
    fresh_grid = fresh_key_value.reshape(N_SRC, DECODE_SLOTS, DECODE_STEPS, 2 * KEY_VALUE_HEADS * HEAD_SIZE)
    in_queries = query_grid[:, :REPLICA_REQUESTS].reshape(INCOMING_TOTAL, DECODE_STEPS, QUERY_HEADS * HEAD_SIZE)
    incoming_fresh = fresh_grid[:, :REPLICA_REQUESTS].reshape(INCOMING_TOTAL, DECODE_STEPS, 2 * KEY_VALUE_HEADS * HEAD_SIZE)
    res_queries = query_grid[:, REPLICA_REQUESTS:].reshape(RESIDENT_TOTAL, DECODE_STEPS, QUERY_HEADS * HEAD_SIZE)
    resident_fresh = fresh_grid[:, REPLICA_REQUESTS:].reshape(RESIDENT_TOTAL, DECODE_STEPS, 2 * KEY_VALUE_HEADS * HEAD_SIZE)

    def attend_pack(packed):
        return attend_one(packed[0], packed[1], packed[2], packed[3])
    in_out = lax.map(attend_pack, (in_queries, in_cache, slot_len, incoming_fresh))
    res_out = lax.map(attend_pack, (res_queries, res_cache, res_len, resident_fresh))
    attention = jnp.concatenate([in_out.reshape(N_SRC, REPLICA_REQUESTS, DECODE_STEPS, QUERY_HEADS * HEAD_SIZE), res_out.reshape(N_SRC, RR, DECODE_STEPS, QUERY_HEADS * HEAD_SIZE)], axis=1)
    return (in_cache, attention.reshape(N_SRC * DECODE_SLOTS, DECODE_STEPS, QUERY_HEADS * HEAD_SIZE))
```

```python
import functools
import itertools
import math

import jax
import jax.numpy as jnp
from jax import lax
from jax.experimental import pallas as pl
from jax.experimental.pallas import tpu as pltpu
from jax.sharding import PartitionSpec as P

QUERY_HEADS = 64
KEY_VALUE_HEADS = 8
HEAD_SIZE = 128
GROUP = 16
N_SRC = 4
N_SEQ = 32
FEAT = 2048
KEY_WIDTH = KEY_VALUE_HEADS * HEAD_SIZE
MESH = pl.DeviceIdType.MESH
MIB = 2**20


def orbit(offset):
    y, x, z, core = offset
    found = []
    for sign in (1, -1):
        for turned in ((y, x, z), (z, y, x), (x, z, y)):
            found.append(tuple((sign * v) % 4 for v in turned) + (core,))
    return found


def send_offsets():
    every = [o for o in itertools.product(range(4), range(4), range(4), range(2)) if any(o)]
    hops = lambda o: sum(min(v, 4 - v) for v in o[:3])
    ordered = []
    for offset in sorted(every, key=lambda o: -hops(o)):
        for turned in orbit(offset):
            if turned not in ordered:
                ordered.append(turned)
    mixed = []
    for near in range(64):
        mixed.append(ordered[near])
        mixed.append(ordered[126 - near])
    return list(dict.fromkeys(mixed))


OFFSETS = send_offsets()


def own_place():
    src = lax.axis_index("src")
    seq = lax.axis_index("seq")
    return src, seq // 8, lax.rem(seq // 2, 4), lax.rem(seq, 2)


def place_at(own, offset):
    src, x, z, core = own
    dy, dx, dz, dcore = offset
    to_src = lax.rem(src + dy, 4) if dy else src
    to_x = lax.rem(x + dx, 4) if dx else x
    to_z = lax.rem(z + dz, 4) if dz else z
    to_core = 1 - core if dcore else core
    return to_src, to_x * 8 + to_z * 2 + to_core


WINDOW = 32


def move_kernel(
    assign, delta_hbm, anchors_hbm, scales_hbm, recv_hbm,
    delta, anchors, scales, anchor_rows, scale_rows, rebuilt,
    load_sem, own_sem, send_sem, recv_sem,
):
    own = own_place()
    src, seq = lax.axis_index("src"), lax.axis_index("seq")
    loads = [
        pltpu.make_async_copy(anchors_hbm, anchors, load_sem.at[0]),
        pltpu.make_async_copy(scales_hbm, scales, load_sem.at[1]),
        pltpu.make_async_copy(delta_hbm, delta, load_sem.at[2]),
    ]
    for load in loads:
        load.start()
    barrier = pltpu.get_barrier_semaphore()
    for offset in OFFSETS:
        pl.semaphore_signal(barrier, inc=1, device_id=place_at(own, offset), device_id_type=MESH)
    for load in loads:
        load.wait()
    for target in range(N_SRC):
        request = jnp.int32(0)
        for local in range(4):
            slot = assign[src * 4 + local]
            here = jnp.logical_and(slot >= target * 4, slot < target * 4 + 4)
            request = jnp.where(here, local, request)
        anchor_rows[...] = anchors[request].astype(jnp.float32)
        scale = scales[request]
        for head in range(FEAT // HEAD_SIZE):
            scale_rows[:, head * HEAD_SIZE : (head + 1) * HEAD_SIZE] = jnp.broadcast_to(
                scale[:, head : head + 1], (N_SEQ, HEAD_SIZE)
            )

        @pl.loop(0, N_SEQ)
        def _(group):
            rows = anchor_rows[pl.ds(group, 1), :] + scale_rows[pl.ds(group, 1), :] * delta[
                request, group
            ].astype(jnp.float32)
            rebuilt[target * N_SEQ + group] = rows.astype(jnp.bfloat16)

    mine = src * N_SEQ + seq
    keep = pltpu.make_async_copy(rebuilt.at[mine], recv_hbm.at[mine], own_sem)
    keep.start()
    pl.semaphore_wait(barrier, len(OFFSETS))
    copies = []
    for half in range(2):
        columns = pl.ds(half * (FEAT // 2), FEAT // 2)
        for offset in OFFSETS:
            to_src, to_seq = place_at(own, offset)
            number = len(copies)
            if number >= WINDOW:
                copies[number - WINDOW].wait_send()
            copy = pltpu.make_async_remote_copy(
                src_ref=rebuilt.at[to_src * N_SEQ + to_seq, :, columns],
                dst_ref=recv_hbm.at[mine, :, columns],
                send_sem=send_sem.at[number % WINDOW],
                recv_sem=recv_sem,
                device_id=(to_src, to_seq),
                device_id_type=MESH,
            )
            copy.start()
            copies.append(copy)
    for copy in copies[-WINDOW:]:
        copy.wait_send()
    arrived = recv_hbm.at[pl.ds(0, len(OFFSETS))]
    pltpu.make_async_copy(arrived, arrived, recv_sem).wait()
    keep.wait()


def move(assign, delta, anchors, scales):
    any_space = pl.BlockSpec(memory_space=pl.ANY)
    return pl.pallas_call(
        move_kernel,
        out_shape=jax.ShapeDtypeStruct((N_SRC * N_SEQ, GROUP, FEAT), jnp.bfloat16),
        in_specs=[pl.BlockSpec(memory_space=pltpu.SMEM)] + [any_space] * 3,
        out_specs=any_space,
        scratch_shapes=[
            pltpu.VMEM((4, N_SEQ, GROUP, FEAT), jnp.bfloat16),
            pltpu.VMEM((4, N_SEQ, FEAT), jnp.bfloat16),
            pltpu.VMEM((4, N_SEQ, FEAT // HEAD_SIZE), jnp.float32),
            pltpu.VMEM((N_SEQ, FEAT), jnp.float32),
            pltpu.VMEM((N_SEQ, FEAT), jnp.float32),
            pltpu.VMEM((N_SRC * N_SEQ, GROUP, FEAT), jnp.bfloat16),
            pltpu.SemaphoreType.DMA((3,)),
            pltpu.SemaphoreType.DMA,
            pltpu.SemaphoreType.DMA((WINDOW,)),
            pltpu.SemaphoreType.DMA,
        ],
        compiler_params=pltpu.CompilerParams(
            collective_id=1, has_side_effects=True, vmem_limit_bytes=48 * MIB
        ),
    )(assign, delta, anchors, scales)


SPAN = N_SEQ * GROUP
PLACE_ROWS = 256


def place_kernel(table, recv, out):
    slot, block = pl.program_id(0), pl.program_id(1)
    row = lax.broadcasted_iota(jnp.int32, (PLACE_ROWS, FEAT), 0)
    live = row < table[4 + slot] - block * PLACE_ROWS
    out[...] = jnp.where(live[None], recv[...], jnp.zeros_like(recv))


def place(table, recv):
    block = (1, PLACE_ROWS, FEAT)
    return pl.pallas_call(
        place_kernel,
        out_shape=jax.ShapeDtypeStruct((4, SPAN, FEAT), jnp.bfloat16),
        grid_spec=pltpu.PrefetchScalarGridSpec(
            num_scalar_prefetch=1,
            grid=(4, SPAN // PLACE_ROWS),
            in_specs=[pl.BlockSpec(block, lambda slot, part, table: (table[slot], part, 0))],
            out_specs=pl.BlockSpec(block, lambda slot, part, table: (slot, part, 0)),
        ),
        compiler_params=pltpu.CompilerParams(vmem_limit_bytes=32 * MIB),
    )(table, recv)


def partial_state(query_head_list, cached_row_list, valid_mask):
    slots = query_head_list.shape[0]
    keys = cached_row_list[:, :, :KEY_WIDTH].reshape(slots, -1, KEY_VALUE_HEADS, HEAD_SIZE)
    values = cached_row_list[:, :, KEY_WIDTH:].reshape(slots, -1, KEY_VALUE_HEADS, HEAD_SIZE)
    scores = jnp.einsum(
        "nhrd,nthd->nhrt", query_head_list, keys, preferred_element_type=jnp.float32
    ) / math.sqrt(HEAD_SIZE)
    keep_mask = valid_mask[:, None, None, :]
    scores = jnp.where(keep_mask, scores, -1e30)
    row_peak = jnp.max(scores, axis=-1)
    weights = jnp.where(keep_mask, jnp.exp(scores - row_peak[..., None]), 0.0)
    row_total = jnp.sum(weights, axis=-1)
    summed = jnp.einsum(
        "nhrt,nthd->nhrd", weights.astype(jnp.bfloat16), values, preferred_element_type=jnp.float32
    )
    return row_peak, row_total, summed


def on_device(
    kv_delta, anchors, scales, in_len, assign, res_cache, res_len, queries, fresh_key_value
):
    src = lax.axis_index("src")
    seq = lax.axis_index("seq")
    recv = move(
        assign,
        kv_delta.reshape(4, N_SEQ, GROUP, FEAT),
        anchors.reshape(4, N_SEQ, FEAT),
        scales.reshape(4, N_SEQ, FEAT // HEAD_SIZE),
    )
    slot_ids = src * 4 + jnp.arange(4)
    matches = assign[:, None] == slot_ids[None, :]
    slot_len = jnp.sum(jnp.where(matches, in_len[:, None], 0), axis=0)
    from_src = jnp.sum(jnp.where(matches, (jnp.arange(16) // 4)[:, None], 0), axis=0)
    table = jnp.concatenate([from_src, slot_len - seq * SPAN]).astype(jnp.int32)
    in_cache = place(table, recv.reshape(4, SPAN, FEAT))

    heads = queries.reshape(8, 4, KEY_VALUE_HEADS, 8, HEAD_SIZE).transpose(0, 2, 1, 3, 4)
    heads = heads.reshape(8, KEY_VALUE_HEADS, 32, HEAD_SIZE)
    res_own = lax.dynamic_slice_in_dim(res_len, src * 4, 4)
    in_valid = (seq * SPAN + jnp.arange(SPAN))[None, :] < slot_len[:, None]
    res_valid = (seq * 256 + jnp.arange(256))[None, :] < res_own[:, None]
    incoming = partial_state(heads[:4], in_cache, in_valid)
    resident = partial_state(heads[4:], res_cache, res_valid)
    peak, total, summed = [
        jnp.concatenate(pair, axis=0).reshape((N_SEQ, 64) + pair[0].shape[3:])
        for pair in zip(incoming, resident)
    ]
    stats = jnp.stack([peak, total], axis=1)
    stats, summed = [lax.all_to_all(a, "seq", 0, 0, tiled=True) for a in (stats, summed)]
    top = jnp.max(stats[:, 0], axis=0)
    factor = jnp.exp(stats[:, 0] - top)
    total = jnp.sum(stats[:, 1] * factor, axis=0)
    summed = jnp.sum(summed * factor[..., None], axis=0)
    row_peak, row_total, summed = [lax.all_gather(a, "seq") for a in (top, total, summed)]
    row_peak = row_peak.reshape(8, 8, 4, 8)
    row_total = row_total.reshape(8, 8, 4, 8)
    summed = summed.reshape(8, 8, 4, 8, HEAD_SIZE)

    query_head_list = queries.reshape(8, 4, KEY_VALUE_HEADS, 8, HEAD_SIZE)
    fresh_keys = fresh_key_value[:, :, :KEY_WIDTH].reshape(8, 4, KEY_VALUE_HEADS, HEAD_SIZE)
    fresh_values = fresh_key_value[:, :, KEY_WIDTH:].reshape(8, 4, KEY_VALUE_HEADS, HEAD_SIZE)
    new_scores = jnp.einsum(
        "nshgd,nthd->nhsgt", query_head_list, fresh_keys, preferred_element_type=jnp.float32
    ) / math.sqrt(HEAD_SIZE)
    causal = (jnp.arange(4)[None, :] <= jnp.arange(4)[:, None])[None, None, :, None, :]
    new_scores = jnp.where(causal, new_scores, -1e30)
    top_score = jnp.maximum(row_peak, jnp.max(new_scores, axis=-1))
    old_factor = jnp.exp(row_peak - top_score)
    new_weights = jnp.where(causal, jnp.exp(new_scores - top_score[..., None]), 0.0)
    row_total = row_total * old_factor + jnp.sum(new_weights, axis=-1)
    summed = summed * old_factor[..., None] + jnp.einsum(
        "nhsgt,nthd->nhsgd",
        new_weights.astype(jnp.bfloat16),
        fresh_values,
        preferred_element_type=jnp.float32,
    )
    result = (summed / row_total[..., None]).transpose(0, 2, 1, 3, 4).reshape(8, 4, -1)
    return in_cache, result.astype(jnp.bfloat16)


def solution(mesh):
    in_specs = (
        P("src", None, "seq", None, None),
        P("src", None, "seq", None),
        P("src", None, "seq", None),
        P(),
        P(),
        P("src", "seq", None),
        P(),
        P("src", None, None),
        P("src", None, None),
    )
    out_specs = (P("src", "seq", None), P("src", None, None))
    return jax.shard_map(
        on_device, mesh=mesh, in_specs=in_specs, out_specs=out_specs, check_vma=False
    )
```

```python
import functools
import itertools
import math

import jax
import jax.numpy as jnp
from jax import lax
from jax.experimental import pallas as pl
from jax.experimental.pallas import tpu as pltpu
from jax.sharding import PartitionSpec as P

QUERY_HEADS = 64
KEY_VALUE_HEADS = 8
HEAD_SIZE = 128
GROUP = 16
N_SRC = 4
N_SEQ = 32
FEAT = 2048
KEY_WIDTH = KEY_VALUE_HEADS * HEAD_SIZE
MESH = pl.DeviceIdType.MESH
MIB = 2**20


def orbit(offset):
    y, x, z, core = offset
    found = []
    for sign in (1, -1):
        for turned in ((y, x, z), (z, y, x), (x, z, y)):
            found.append(tuple((sign * v) % 4 for v in turned) + (core,))
    return found


def send_offsets():
    every = [o for o in itertools.product(range(4), range(4), range(4), range(2)) if any(o)]
    hops = lambda o: sum(min(v, 4 - v) for v in o[:3])
    ordered = []
    for offset in sorted(every, key=lambda o: -hops(o)):
        for turned in orbit(offset):
            if turned not in ordered:
                ordered.append(turned)
    mixed = []
    for near in range(64):
        mixed.append(ordered[near])
        mixed.append(ordered[126 - near])
    return list(dict.fromkeys(mixed))


OFFSETS = send_offsets()


def own_place():
    src = lax.axis_index("src")
    seq = lax.axis_index("seq")
    return src, seq // 8, lax.rem(seq // 2, 4), lax.rem(seq, 2)


def place_at(own, offset):
    src, x, z, core = own
    dy, dx, dz, dcore = offset
    to_src = lax.rem(src + dy, 4) if dy else src
    to_x = lax.rem(x + dx, 4) if dx else x
    to_z = lax.rem(z + dz, 4) if dz else z
    to_core = 1 - core if dcore else core
    return to_src, to_x * 8 + to_z * 2 + to_core

SPAN = N_SEQ * GROUP
RES_SPAN = 256
ROWS = 32
QUERY_ROWS = KEY_VALUE_HEADS * ROWS
CARD = QUERY_ROWS + KEY_VALUE_HEADS * GROUP
LOWEST = -1e30
WINDOW = 200
PUMP_BLOCK, PUMP_CORE, PUMP_PAIR, PUMP_RESULT = 4, 4, 8, 4
PLANE_OFFSETS = [o for o in OFFSETS if o[0] == 0 and o[3] == 0]
PLANE = 16


def remote(src_ref, dst_ref, send_sem, recv_sem, place):
    return pltpu.make_async_remote_copy(
        src_ref=src_ref,
        dst_ref=dst_ref,
        send_sem=send_sem,
        recv_sem=recv_sem,
        device_id=place,
        device_id_type=MESH,
    )


def take_bytes(ref, sem):
    pltpu.make_async_copy(ref, ref, sem).wait()


def partial_of(card, cache_keys, cache_values, live, first, head):
    query = card[pl.ds(pl.multiple_of(head * ROWS, ROWS), ROWS), :]
    fresh = card[pl.ds(pl.multiple_of(QUERY_ROWS + head * GROUP, GROUP), GROUP), :]
    across = (((1,), (1,)), ((), ()))
    unit = 1.0 / math.sqrt(HEAD_SIZE)
    scores = lax.dot_general(query, cache_keys, across, preferred_element_type=jnp.float32) * unit
    new_scores = lax.dot_general(query, fresh, across, preferred_element_type=jnp.float32) * unit
    step = lax.broadcasted_iota(jnp.int32, (ROWS, GROUP), 0) % 4
    token = lax.broadcasted_iota(jnp.int32, (ROWS, GROUP), 1)
    new_live = jnp.logical_and(token <= step, first)
    scores = jnp.where(live, scores, LOWEST)
    new_scores = jnp.where(new_live, new_scores, LOWEST)
    peak = jnp.maximum(
        jnp.max(scores, axis=1, keepdims=True), jnp.max(new_scores, axis=1, keepdims=True)
    )
    weights = jnp.where(live, jnp.exp(scores - peak), 0.0)
    new_weights = jnp.where(new_live, jnp.exp(new_scores - peak), 0.0)
    total = jnp.sum(weights, axis=1, keepdims=True) + jnp.sum(new_weights, axis=1, keepdims=True)
    summed = jnp.dot(
        weights.astype(jnp.bfloat16), cache_values, preferred_element_type=jnp.float32
    )
    rounded = new_weights.astype(jnp.bfloat16).astype(jnp.float32)
    fresh = fresh.astype(jnp.float32)
    for new in range(4):
        summed = summed + rounded[:, new : new + 1] * fresh[4 + new : 5 + new, :]
    return peak, total, summed


def read_cards(queries, fresh, cards):
    @pl.loop(0, 8)
    def _(slot):
        asked = queries[slot].astype(jnp.float32)
        new = fresh[slot].astype(jnp.float32)
        for head in range(KEY_VALUE_HEADS):
            rows = [
                asked[:, column * HEAD_SIZE : (column + 1) * HEAD_SIZE]
                for column in range(head * 8, head * 8 + 8)
            ]
            cards[slot, head * ROWS : (head + 1) * ROWS, :] = jnp.concatenate(
                rows, axis=0
            ).astype(jnp.bfloat16)
            low = head * HEAD_SIZE
            rows = [
                new[:, low : low + HEAD_SIZE],
                new[:, KEY_WIDTH + low : KEY_WIDTH + low + HEAD_SIZE],
                jnp.zeros((8, HEAD_SIZE), jnp.float32),
            ]
            begin = QUERY_ROWS + head * GROUP
            cards[slot, begin : begin + GROUP, :] = jnp.concatenate(rows, axis=0).astype(
                jnp.bfloat16
            )


def move_kernel(
    assign_hbm, in_len_hbm, res_len_hbm, delta_hbm, anchors_hbm, scales_hbm, resident_hbm, queries_hbm,
    fresh_hbm, recv_hbm, result_out,
    assign, in_len, res_len, delta, anchors, scales, resident, queries, fresh, cards, anchor_rows, scale_rows, rebuilt,
    cards_out, cards_in, part_out, stat_out, core_part, core_stat, joint_part, joint_stat,
    part_in, stat_in, factors, result, unused,
    load_sem, own_sem, send_sem, recv_sem, card_send, card_recv, core_send, core_recv,
    pair_send, pair_recv, result_send, result_recv, back_send, back_recv,
):
    own = own_place()
    src, seq = lax.axis_index("src"), lax.axis_index("seq")
    x, z, core = own[1:]
    plane = x * 4 + z
    sibling = (src, seq + 1 - 2 * core)
    loads = [
        pltpu.make_async_copy(anchors_hbm, anchors, load_sem.at[0]),
        pltpu.make_async_copy(scales_hbm, scales, load_sem.at[1]),
        pltpu.make_async_copy(delta_hbm, delta, load_sem.at[2]),
        pltpu.make_async_copy(queries_hbm, queries, load_sem.at[3]),
        pltpu.make_async_copy(fresh_hbm, fresh, load_sem.at[4]),
        pltpu.make_async_copy(resident_hbm, resident, load_sem.at[5]),
        pltpu.make_async_copy(assign_hbm, assign, load_sem.at[6]),
        pltpu.make_async_copy(in_len_hbm, in_len, load_sem.at[7]),
        pltpu.make_async_copy(res_len_hbm, res_len, load_sem.at[8]),
    ]
    for load in loads:
        load.start()
    barrier = pltpu.get_barrier_semaphore()
    for offset in OFFSETS:
        pl.semaphore_signal(barrier, inc=1, device_id=place_at(own, offset), device_id_type=MESH)
    for load in loads[:3] + loads[6:]:
        load.wait()
    same_group = lax.broadcasted_iota(jnp.int32, (N_SEQ, N_SEQ), 0) == lax.broadcasted_iota(
        jnp.int32, (N_SEQ, N_SEQ), 1
    )
    lengths = []
    for target in range(N_SRC):
        request, length = jnp.int32(0), jnp.int32(0)
        for local in range(4):
            slot = assign[src * 4 + local]
            here = jnp.logical_and(slot >= target * 4, slot < target * 4 + 4)
            request = jnp.where(here, local, request)
            length = jnp.where(here, in_len[src * 4 + local], length)
        lengths.append(length)
        anchor_rows[...] = anchors[request].astype(jnp.float32)
        scale = scales[request]
        for head in range(FEAT // HEAD_SIZE):
            column = jnp.sum(
                jnp.where(same_group, scale[head : head + 1, :], 0.0), axis=1, keepdims=True
            )
            scale_rows[:, head * HEAD_SIZE : (head + 1) * HEAD_SIZE] = jnp.broadcast_to(
                column, (N_SEQ, HEAD_SIZE)
            )

        @pl.loop(0, N_SEQ)
        def _(group):
            rows = anchor_rows[pl.ds(group, 1), :] + scale_rows[pl.ds(group, 1), :] * delta[
                request, group
            ].reshape(GROUP, FEAT).astype(jnp.float32)
            rebuilt[target, pl.ds(pl.multiple_of(group * GROUP, GROUP), GROUP), :] = rows.astype(
                jnp.bfloat16
            )

    for load in loads[3:5]:
        load.wait()
    read_cards(queries, fresh, cards)
    for source in range(N_SRC):
        place = jnp.int32(0)
        for local in range(4):
            slot = assign[source * 4 + local] - src * 4
            place = jnp.where(jnp.logical_and(slot >= 0, slot < 4), slot, place)
        cards_out[source] = cards[place]
    cards_in[src] = cards_out[src]

    mine = src * N_SEQ + seq
    keep = pltpu.make_async_copy(
        rebuilt.at[src, pl.ds(pl.multiple_of(seq * GROUP, GROUP), GROUP), :],
        recv_hbm.at[mine],
        own_sem,
    )
    keep.start()
    pl.semaphore_wait(barrier, len(OFFSETS))

    card_copies = []
    for turn in range(1, N_SRC):
        to_src = lax.rem(src + turn, N_SRC)
        card_copies.append(
            remote(
                cards_out.at[to_src], cards_in.at[src],
                card_send.at[turn - 1], card_recv.at[turn - 1], (to_src, seq),
            )
        )
        card_copies[-1].start()

    copies = []
    work = [(half, offset) for half in range(2) for offset in OFFSETS]

    def pump(count):
        for half, offset in work[len(copies) : len(copies) + count]:
            to_src, to_seq = place_at(own, offset)
            columns = pl.ds(half * (FEAT // 2), FEAT // 2)
            number = len(copies)
            if number >= WINDOW:
                copies[number - WINDOW].wait_send()
            copy = remote(
                rebuilt.at[to_src, pl.ds(pl.multiple_of(to_seq * GROUP, GROUP), GROUP), columns],
                recv_hbm.at[mine, :, columns],
                send_sem.at[number % WINDOW],
                recv_sem,
                (to_src, to_seq),
            )
            copy.start()
            copies.append(copy)

    pump(WINDOW)
    for copy in card_copies:
        copy.wait()
    loads[5].wait()

    first = seq == 0
    ahead = lax.broadcasted_iota(jnp.int32, (1, SPAN), 1)
    in_position = ahead // GROUP * SPAN + seq * GROUP + ahead % GROUP
    res_position = seq * RES_SPAN + lax.broadcasted_iota(jnp.int32, (1, RES_SPAN), 1)
    row_id = lax.broadcasted_iota(jnp.int32, (ROWS, HEAD_SIZE), 0)
    lane_id = lax.broadcasted_iota(jnp.int32, (ROWS, HEAD_SIZE), 1)
    for block in range(4):
        in_live = in_position < lengths[block]
        res_live = res_position < res_len[src * 4 + block]
        for start in (0, 4):

            @pl.loop(start, start + 4)
            def _(head):
                keys = pl.ds(pl.multiple_of(head * HEAD_SIZE, HEAD_SIZE), HEAD_SIZE)
                values = pl.ds(pl.multiple_of(KEY_WIDTH + head * HEAD_SIZE, HEAD_SIZE), HEAD_SIZE)
                in_peak, in_total, in_sum = partial_of(
                    cards_in.at[block], rebuilt[block, :, keys], rebuilt[block, :, values],
                    in_live, first, head,
                )
                res_peak, res_total, res_sum = partial_of(
                    cards.at[4 + block], resident[block, :, keys], resident[block, :, values],
                    res_live, first, head,
                )
                to_core, to_plane = head % 2, block * 4 + head // 2
                part_out[to_core, to_plane, 0] = in_sum.astype(jnp.bfloat16)
                part_out[to_core, to_plane, 1] = res_sum.astype(jnp.bfloat16)
                held = jnp.where(
                    lane_id < 64,
                    jnp.where(lane_id < 32, in_peak, in_total),
                    jnp.where(lane_id < 96, res_peak, res_total),
                )
                stat_out[to_core, to_plane] = jnp.sum(
                    jnp.where(lane_id % ROWS == row_id, held, 0.0), axis=0, keepdims=True
                )

            pump(PUMP_BLOCK)

    core_copies = [
        remote(
            stat_out.at[1 - core], core_stat, core_send.at[0], core_recv.at[0], sibling
        ),
        remote(
            part_out.at[1 - core], core_part, core_send.at[1], core_recv.at[1], sibling
        ),
    ]
    for copy in core_copies:
        copy.start()
    pump(PUMP_CORE)
    for copy in core_copies:
        copy.wait()

    def columns_of(row):
        return [
            jnp.sum(jnp.where(lane_id == row_id + lane, row, 0.0), axis=1, keepdims=True)
            for lane in (0, 64)
        ]

    stat_lane = lax.broadcasted_iota(jnp.int32, (1, HEAD_SIZE), 1)
    is_peak = stat_lane % 64 < 32

    @pl.loop(0, PLANE)
    def _(pair):
        here, there = stat_out[core, pair], core_stat[pair]
        peak = jnp.maximum(here, there)
        here_factor, there_factor = jnp.exp(here - peak), jnp.exp(there - peak)
        total = here * pltpu.roll(here_factor, ROWS, 1) + there * pltpu.roll(there_factor, ROWS, 1)
        joint_stat[pair] = jnp.where(is_peak, peak, total)
        here_columns, there_columns = columns_of(here_factor), columns_of(there_factor)
        for kind in range(2):
            joint_part[pair, kind] = (
                here_columns[kind] * part_out[core, pair, kind].astype(jnp.float32)
                + there_columns[kind] * core_part[pair, kind].astype(jnp.float32)
            ).astype(jnp.bfloat16)

    part_in[plane] = joint_part[plane]
    stat_in[plane] = joint_stat[plane]
    for offset in PLANE_OFFSETS:
        place = place_at(own, offset)
        to_plane = place[1] // 2
        remote(
            joint_stat.at[to_plane], stat_in.at[plane], pair_send.at[0], pair_recv.at[0], place
        ).start()
        remote(
            joint_part.at[to_plane], part_in.at[plane], pair_send.at[1], pair_recv.at[1], place
        ).start()
    pump(PUMP_PAIR)
    others = pl.ds(0, PLANE - 1)
    take_bytes(stat_in.at[others], pair_recv.at[0])
    take_bytes(part_in.at[others], pair_recv.at[1])
    stats = jnp.concatenate([stat_in[device] for device in range(PLANE)], axis=0)
    factor = jnp.exp(stats - jnp.max(stats, axis=0, keepdims=True))
    totals = pltpu.roll(stats, HEAD_SIZE - ROWS, 1)
    factors[...] = factor / jnp.sum(factor * totals, axis=0, keepdims=True)

    def add(device, sums):
        columns = columns_of(factors[pl.ds(device, 1), :])
        return tuple(
            sums[kind] + columns[kind] * part_in[device, kind].astype(jnp.float32)
            for kind in range(2)
        )

    zero = jnp.zeros((ROWS, HEAD_SIZE), jnp.float32)
    sums = lax.fori_loop(0, PLANE, add, (zero, zero))
    for kind in range(2):
        result[kind] = sums[kind].astype(jnp.bfloat16)

    row = src * 4 + z
    at_home = pltpu.make_async_copy(result.at[1], result_out.at[1, core, plane], own_sem)

    @pl.when(x == src)
    def _():
        pltpu.make_async_copy(result.at[0], result_out.at[0, core, row], result_recv.at[0]).start()
        pltpu.make_async_copy(result.at[0], unused, result_send.at[0]).start()

    @pl.when(x != src)
    def _():
        remote(
            result.at[0], result_out.at[0, core, row], result_send.at[0], result_recv.at[0],
            (x, seq),
        ).start()

    for offset in PLANE_OFFSETS:
        to_seq = place_at(own, offset)[1]
        remote(
            result.at[0], result_out.at[0, core, row], result_send.at[0], result_recv.at[0],
            (x, to_seq),
        ).start()
        remote(
            result.at[1], result_out.at[1, core, plane], result_send.at[1], result_recv.at[1],
            (src, to_seq),
        ).start()
    keep.wait()
    at_home.start()
    pump(PUMP_RESULT)
    at_home.wait()
    take_bytes(result_out.at[0, core], result_recv.at[0])
    take_bytes(result_out.at[1, core, others], result_recv.at[1])
    back_copies = [
        remote(
            result_out.at[kind, core], result_out.at[kind, core],
            back_send.at[kind], back_recv.at[kind], sibling,
        )
        for kind in range(2)
    ]
    for copy in back_copies:
        copy.start()
    pump(len(work))
    take_bytes(stat_in.at[others], pair_send.at[0])
    take_bytes(part_in.at[others], pair_send.at[1])
    take_bytes(result_out.at[0, core], result_send.at[0])
    take_bytes(result_out.at[1, core, others], result_send.at[1])
    for copy in back_copies:
        copy.wait()
    for copy in copies[-WINDOW:]:
        copy.wait_send()
    take_bytes(recv_hbm.at[pl.ds(0, len(OFFSETS))], recv_sem)


def move(assign, in_len, res_len, delta, anchors, scales, resident, queries, fresh):
    any_space = pl.BlockSpec(memory_space=pl.ANY)
    bf16, f32 = jnp.bfloat16, jnp.float32
    operands = [
        pltpu.with_memory_space_constraint(a, pltpu.HBM)
        for a in (assign, in_len, res_len, delta, anchors, scales, resident, queries, fresh)
    ]
    return pl.pallas_call(
        move_kernel,
        out_shape=(
            pltpu.VMEM((N_SRC * N_SEQ, GROUP, FEAT), bf16),
            pltpu.VMEM((2, 2, PLANE, ROWS, HEAD_SIZE), bf16),
        ),
        in_specs=[pl.BlockSpec(memory_space=pltpu.HBM)] * 9,
        out_specs=(any_space, any_space),
        scratch_shapes=[
            pltpu.SMEM((16,), jnp.int32),
            pltpu.SMEM((16,), jnp.int32),
            pltpu.SMEM((16,), jnp.int32),
            pltpu.VMEM(delta.shape, bf16),
            pltpu.VMEM(anchors.shape, bf16),
            pltpu.VMEM(scales.shape, f32),
            pltpu.VMEM(resident.shape, bf16),
            pltpu.VMEM(queries.shape, bf16),
            pltpu.VMEM(fresh.shape, bf16),
            pltpu.VMEM((8, CARD, HEAD_SIZE), bf16),
            pltpu.VMEM((N_SEQ, FEAT), f32),
            pltpu.VMEM((N_SEQ, FEAT), f32),
            pltpu.VMEM((N_SRC, SPAN, FEAT), bf16),
            pltpu.VMEM((N_SRC, CARD, HEAD_SIZE), bf16),
            pltpu.VMEM((N_SRC, CARD, HEAD_SIZE), bf16),
            pltpu.VMEM((2, PLANE, 2, ROWS, HEAD_SIZE), bf16),
            pltpu.VMEM((2, PLANE, 1, HEAD_SIZE), f32),
            pltpu.VMEM((PLANE, 2, ROWS, HEAD_SIZE), bf16),
            pltpu.VMEM((PLANE, 1, HEAD_SIZE), f32),
            pltpu.VMEM((PLANE, 2, ROWS, HEAD_SIZE), bf16),
            pltpu.VMEM((PLANE, 1, HEAD_SIZE), f32),
            pltpu.VMEM((PLANE, 2, ROWS, HEAD_SIZE), bf16),
            pltpu.VMEM((PLANE, 1, HEAD_SIZE), f32),
            pltpu.VMEM((PLANE, HEAD_SIZE), f32),
            pltpu.VMEM((2, ROWS, HEAD_SIZE), bf16),
            pltpu.VMEM((ROWS, HEAD_SIZE), bf16),
            pltpu.SemaphoreType.DMA((9,)),
            pltpu.SemaphoreType.DMA,
            pltpu.SemaphoreType.DMA((WINDOW,)),
            pltpu.SemaphoreType.DMA,
            pltpu.SemaphoreType.DMA((3,)),
            pltpu.SemaphoreType.DMA((3,)),
            pltpu.SemaphoreType.DMA((2,)),
            pltpu.SemaphoreType.DMA((2,)),
            pltpu.SemaphoreType.DMA((2,)),
            pltpu.SemaphoreType.DMA((2,)),
            pltpu.SemaphoreType.DMA((2,)),
            pltpu.SemaphoreType.DMA((2,)),
            pltpu.SemaphoreType.DMA((2,)),
            pltpu.SemaphoreType.DMA((2,)),
        ],
        compiler_params=pltpu.CompilerParams(
            collective_id=1, has_side_effects=True, vmem_limit_bytes=32 * MIB
        ),
    )(*operands)


EDGE = 64


def place_kernel(
    assign_hbm, in_len_hbm, recv, result, in_cache, attention,
    assign, in_len, zeros, edge, out_sem, edge_sem, load_sem,
):
    src, seq = lax.axis_index("src"), lax.axis_index("seq")
    loads = [
        pltpu.make_async_copy(assign_hbm, assign, load_sem.at[0]),
        pltpu.make_async_copy(in_len_hbm, in_len, load_sem.at[1]),
    ]
    for load in loads:
        load.start()
    for load in loads:
        load.wait()
    zeros[...] = jnp.zeros_like(zeros)
    sources, counts = [], []
    for slot in range(4):
        source, length = jnp.int32(0), jnp.int32(0)
        for request in range(16):
            here = assign[request] == src * 4 + slot
            source = jnp.where(here, request // 4, source)
            length = jnp.where(here, in_len[request], length)
        count = jnp.clip(length - seq * SPAN, 0, SPAN)
        sources.append(source)
        counts.append(count)
        whole = count // EDGE
        cut = whole * EDGE < count
        for part in range(SPAN // EDGE):
            rows = pl.ds(part * EDGE, EDGE)

            @pl.when(part < whole)
            def _():
                pltpu.make_async_copy(
                    recv.at[source, rows], in_cache.at[slot, rows], out_sem
                ).start()

            @pl.when(jnp.logical_and(part == whole, cut))
            def _():
                pltpu.make_async_copy(recv.at[source, rows], edge.at[slot], edge_sem.at[slot]).start()

            @pl.when(jnp.logical_and(part >= whole, jnp.logical_or(part > whole, ~cut)))
            def _():
                pltpu.make_async_copy(zeros, in_cache.at[slot, rows], out_sem).start()

    row = lax.broadcasted_iota(jnp.int32, (EDGE, FEAT), 0)
    for slot in range(4):
        whole = counts[slot] // EDGE

        @pl.when(whole * EDGE < counts[slot])
        def _():
            pltpu.make_async_copy(edge.at[slot], edge.at[slot], edge_sem.at[slot]).wait()
            kept = edge[slot]
            edge[slot] = jnp.where(row < counts[slot] - whole * EDGE, kept, jnp.zeros_like(kept))
            rows = pl.ds(pl.multiple_of(whole * EDGE, EDGE), EDGE)
            pltpu.make_async_copy(edge.at[slot], in_cache.at[slot, rows], out_sem).start()

    for slot in range(8):
        for head in range(KEY_VALUE_HEADS):
            first = sources[slot] if slot < 4 else slot - 4
            rows = result[slot // 4, head % 2, first * 4 + head // 2].astype(jnp.float32)
            for column in range(8):
                low = (head * 8 + column) * HEAD_SIZE
                attention[slot, :, low : low + HEAD_SIZE] = rows[
                    column * 4 : column * 4 + 4, :
                ].astype(jnp.bfloat16)
    pltpu.make_async_copy(in_cache, in_cache, out_sem).wait()


def place(assign, in_len, recv, result):
    scalars = pl.BlockSpec(memory_space=pltpu.HBM)
    whole = pl.BlockSpec(memory_space=pltpu.VMEM)
    any_space = pl.BlockSpec(memory_space=pl.ANY)
    return pl.pallas_call(
        place_kernel,
        out_shape=(
            jax.ShapeDtypeStruct((4, SPAN, FEAT), jnp.bfloat16),
            jax.ShapeDtypeStruct((8, 4, QUERY_HEADS * HEAD_SIZE), jnp.bfloat16),
        ),
        in_specs=[scalars, scalars, any_space, whole],
        out_specs=(any_space, whole),
        scratch_shapes=[
            pltpu.SMEM((16,), jnp.int32),
            pltpu.SMEM((16,), jnp.int32),
            pltpu.VMEM((EDGE, FEAT), jnp.bfloat16),
            pltpu.VMEM((4, EDGE, FEAT), jnp.bfloat16),
            pltpu.SemaphoreType.DMA,
            pltpu.SemaphoreType.DMA((4,)),
            pltpu.SemaphoreType.DMA((2,)),
        ],
        compiler_params=pltpu.CompilerParams(vmem_limit_bytes=16 * MIB),
    )(
        pltpu.with_memory_space_constraint(assign, pltpu.HBM),
        pltpu.with_memory_space_constraint(in_len, pltpu.HBM),
        recv,
        result,
    )


def on_device(
    kv_delta, anchors, scales, in_len, assign, res_cache, res_len, queries, fresh_key_value
):
    recv, result = move(
        assign,
        in_len,
        res_len,
        kv_delta.reshape(4, N_SEQ, GROUP, FEAT),
        anchors.reshape(4, N_SEQ, FEAT),
        scales.reshape(4, N_SEQ, FEAT // HEAD_SIZE).transpose(0, 2, 1),
        res_cache,
        queries,
        fresh_key_value,
    )
    return place(assign, in_len, recv.reshape(4, SPAN, FEAT), result)


def solution(mesh):
    in_specs = (
        P("src", None, "seq", None, None),
        P("src", None, "seq", None),
        P("src", None, "seq", None),
        P(),
        P(),
        P("src", "seq", None),
        P(),
        P("src", None, None),
        P("src", None, None),
    )
    out_specs = (P("src", "seq", None), P("src", None, None))
    return jax.shard_map(
        on_device, mesh=mesh, in_specs=in_specs, out_specs=out_specs, check_vma=False
    )
```

```python
import functools
import itertools
import math

import jax
import jax.numpy as jnp
from jax import lax
from jax.experimental import pallas as pl
from jax.experimental.pallas import tpu as pltpu
from jax.sharding import PartitionSpec as P

QUERY_HEADS = 64
KEY_VALUE_HEADS = 8
HEAD_SIZE = 128
GROUP = 16
N_SRC = 4
N_SEQ = 32
FEAT = 2048
KEY_WIDTH = KEY_VALUE_HEADS * HEAD_SIZE
MESH = pl.DeviceIdType.MESH
MIB = 2**20


def orbit(offset):
    y, x, z, core = offset
    found = []
    for sign in (1, -1):
        for turned in ((y, x, z), (z, y, x), (x, z, y)):
            found.append(tuple((sign * v) % 4 for v in turned) + (core,))
    return found


def send_offsets():
    every = [o for o in itertools.product(range(4), range(4), range(4), range(2)) if any(o)]
    hops = lambda o: sum(min(v, 4 - v) for v in o[:3])
    ordered = []
    for offset in sorted(every, key=lambda o: -hops(o)):
        for turned in orbit(offset):
            if turned not in ordered:
                ordered.append(turned)
    mixed = []
    for near in range(64):
        mixed.append(ordered[near])
        mixed.append(ordered[126 - near])
    return list(dict.fromkeys(mixed))


OFFSETS = send_offsets()


def own_place():
    src = lax.axis_index("src")
    seq = lax.axis_index("seq")
    return src, seq // 8, lax.rem(seq // 2, 4), lax.rem(seq, 2)


def place_at(own, offset):
    src, x, z, core = own
    dy, dx, dz, dcore = offset
    to_src = lax.rem(src + dy, 4) if dy else src
    to_x = lax.rem(x + dx, 4) if dx else x
    to_z = lax.rem(z + dz, 4) if dz else z
    to_core = 1 - core if dcore else core
    return to_src, to_x * 8 + to_z * 2 + to_core

SPAN = N_SEQ * GROUP
RES_SPAN = 256
ROWS = 32
QUERY_ROWS = KEY_VALUE_HEADS * ROWS
NEW_ROWS = KEY_VALUE_HEADS * GROUP
LOWEST = -1e30
WINDOW = 170
PUMP_FIRST, PUMP_BLOCK, PUMP_CORE, PUMP_PAIR = 40, 8, 6, 8
PLANE_OFFSETS = [o for o in OFFSETS if o[0] == 0 and o[3] == 0]
PLANE = 16


def remote(src_ref, dst_ref, send_sem, recv_sem, place):
    return pltpu.make_async_remote_copy(
        src_ref=src_ref,
        dst_ref=dst_ref,
        send_sem=send_sem,
        recv_sem=recv_sem,
        device_id=place,
        device_id_type=MESH,
    )


def take_bytes(ref, sem):
    pltpu.make_async_copy(ref, ref, sem).wait()


def partial_of(card, news, cache_keys, cache_values, live, first, head):
    query = card[pl.ds(pl.multiple_of(head * ROWS, ROWS), ROWS), :]
    fresh = news[pl.ds(pl.multiple_of(head * GROUP, GROUP), GROUP), :]
    fresh = jnp.where(first, fresh, jnp.zeros_like(fresh))
    across = (((1,), (1,)), ((), ()))
    unit = 1.0 / math.sqrt(HEAD_SIZE)
    scores = lax.dot_general(query, cache_keys, across, preferred_element_type=jnp.float32) * unit
    new_scores = lax.dot_general(query, fresh, across, preferred_element_type=jnp.float32) * unit
    step = lax.broadcasted_iota(jnp.int32, (ROWS, GROUP), 0) % 4
    token = lax.broadcasted_iota(jnp.int32, (ROWS, GROUP), 1)
    new_live = jnp.logical_and(token <= step, first)
    scores = jnp.where(live, scores, LOWEST)
    new_scores = jnp.where(new_live, new_scores, LOWEST)
    peak = jnp.maximum(
        jnp.max(scores, axis=1, keepdims=True), jnp.max(new_scores, axis=1, keepdims=True)
    )
    weights = jnp.where(live, jnp.exp(scores - peak), 0.0)
    new_weights = jnp.where(new_live, jnp.exp(new_scores - peak), 0.0)
    total = jnp.sum(weights, axis=1, keepdims=True) + jnp.sum(new_weights, axis=1, keepdims=True)
    summed = jnp.dot(
        weights.astype(jnp.bfloat16), cache_values, preferred_element_type=jnp.float32
    )
    rounded = new_weights.astype(jnp.bfloat16).astype(jnp.float32)
    fresh = fresh.astype(jnp.float32)
    for new in range(4):
        summed = summed + rounded[:, new : new + 1] * fresh[4 + new : 5 + new, :]
    return peak, total, summed


def read_cards(queries, fresh, cards, news):
    @pl.loop(0, 8)
    def _(slot):
        asked = queries[slot].astype(jnp.float32)
        new = fresh[slot].astype(jnp.float32)
        for head in range(KEY_VALUE_HEADS):
            rows = [
                asked[:, column * HEAD_SIZE : (column + 1) * HEAD_SIZE]
                for column in range(head * 8, head * 8 + 8)
            ]
            cards[slot, head * ROWS : (head + 1) * ROWS, :] = jnp.concatenate(
                rows, axis=0
            ).astype(jnp.bfloat16)
            low = head * HEAD_SIZE
            rows = [
                new[:, low : low + HEAD_SIZE],
                new[:, KEY_WIDTH + low : KEY_WIDTH + low + HEAD_SIZE],
                jnp.zeros((8, HEAD_SIZE), jnp.float32),
            ]
            news[slot, head * GROUP : (head + 1) * GROUP, :] = jnp.concatenate(
                rows, axis=0
            ).astype(jnp.bfloat16)


def move_kernel(
    assign_hbm, in_len_hbm, res_len_hbm, delta_hbm, anchors_hbm, scales_hbm, resident_hbm, queries_hbm,
    fresh_hbm, recv_hbm, result_out,
    assign, in_len, res_len, delta, anchors, scales, resident, queries, fresh, cards, news, anchor_rows, scale_rows, rebuilt,
    cards_out, cards_in, news_out, news_in, part_out, stat_out, core_part, core_stat, joint_part, joint_stat,
    part_in, stat_in, factors, result, unused,
    load_sem, own_sem, send_sem, recv_sem, card_send, card_recv, new_send, new_recv, swap_send, swap_recv, core_send, core_recv,
    pair_send, pair_recv, result_send, result_recv, back_send, back_recv,
):
    own = own_place()
    src, seq = lax.axis_index("src"), lax.axis_index("seq")
    x, z, core = own[1:]
    plane = x * 4 + z
    sibling = (src, seq + 1 - 2 * core)
    loads = [
        pltpu.make_async_copy(anchors_hbm, anchors, load_sem.at[0]),
        pltpu.make_async_copy(scales_hbm, scales, load_sem.at[1]),
        pltpu.make_async_copy(delta_hbm, delta, load_sem.at[2]),
        pltpu.make_async_copy(queries_hbm, queries, load_sem.at[3]),
        pltpu.make_async_copy(fresh_hbm, fresh, load_sem.at[4]),
        pltpu.make_async_copy(resident_hbm, resident, load_sem.at[5]),
        pltpu.make_async_copy(assign_hbm, assign, load_sem.at[6]),
        pltpu.make_async_copy(in_len_hbm, in_len, load_sem.at[7]),
        pltpu.make_async_copy(res_len_hbm, res_len, load_sem.at[8]),
    ]
    early, late = loads[:3] + loads[6:], loads[3:6]
    for load in early:
        load.start()
    barrier = pltpu.get_barrier_semaphore()
    for offset in OFFSETS:
        pl.semaphore_signal(barrier, inc=1, device_id=place_at(own, offset), device_id_type=MESH)
    for load in late:
        load.start()
    for load in early:
        load.wait()
    same_group = lax.broadcasted_iota(jnp.int32, (N_SEQ, N_SEQ), 0) == lax.broadcasted_iota(
        jnp.int32, (N_SEQ, N_SEQ), 1
    )
    lengths = []
    for target in range(N_SRC):
        request, length = jnp.int32(0), jnp.int32(0)
        for local in range(4):
            slot = assign[src * 4 + local]
            here = jnp.logical_and(slot >= target * 4, slot < target * 4 + 4)
            request = jnp.where(here, local, request)
            length = jnp.where(here, in_len[src * 4 + local], length)
        lengths.append(length)
        anchor_rows[...] = anchors[request].astype(jnp.float32)
        scale = scales[request]
        for head in range(FEAT // HEAD_SIZE):
            column = jnp.sum(
                jnp.where(same_group, scale[head : head + 1, :], 0.0), axis=1, keepdims=True
            )
            scale_rows[:, head * HEAD_SIZE : (head + 1) * HEAD_SIZE] = jnp.broadcast_to(
                column, (N_SEQ, HEAD_SIZE)
            )

        @pl.loop(0, N_SEQ, unroll=2)
        def _(group):
            rows = anchor_rows[pl.ds(group, 1), :] + scale_rows[pl.ds(group, 1), :] * delta[
                request, group
            ].reshape(GROUP, FEAT).astype(jnp.float32)
            rebuilt[target, pl.ds(pl.multiple_of(group * GROUP, GROUP), GROUP), :] = rows.astype(
                jnp.bfloat16
            )

    mine = src * N_SEQ + seq
    keep = pltpu.make_async_copy(
        rebuilt.at[src, pl.ds(pl.multiple_of(seq * GROUP, GROUP), GROUP), :],
        recv_hbm.at[mine],
        own_sem,
    )
    keep.start()
    pl.semaphore_wait(barrier, len(OFFSETS))

    copies = []
    work = [(half, offset) for half in range(2) for offset in OFFSETS]

    def pump(count):
        for half, offset in work[len(copies) : len(copies) + count]:
            to_src, to_seq = place_at(own, offset)
            columns = pl.ds(half * (FEAT // 2), FEAT // 2)
            number = len(copies)
            if number >= WINDOW:
                copies[number - WINDOW].wait_send()
            copy = remote(
                rebuilt.at[to_src, pl.ds(pl.multiple_of(to_seq * GROUP, GROUP), GROUP), columns],
                recv_hbm.at[mine, :, columns],
                send_sem.at[number % WINDOW],
                recv_sem,
                (to_src, to_seq),
            )
            copy.start()
            copies.append(copy)

    pump(PUMP_FIRST)
    for load in late[:2]:
        load.wait()
    read_cards(queries, fresh, cards, news)
    for source in range(N_SRC):
        place = jnp.int32(0)
        for local in range(4):
            slot = assign[source * 4 + local] - src * 4
            place = jnp.where(jnp.logical_and(slot >= 0, slot < 4), slot, place)
        cards_out[source] = cards[place]
        news_out[source] = news[place]
    cards_in[src] = cards_out[src]
    news_in[src] = news_out[src]
    half = pl.ds(pl.multiple_of(core * (QUERY_ROWS // 2), QUERY_ROWS // 2), QUERY_ROWS // 2)
    card_copies, new_copies, swap_copies = [], [], []
    for turn in range(1, N_SRC):
        to_src = lax.rem(src + turn, N_SRC)
        from_src = lax.rem(src + N_SRC - turn, N_SRC)
        card_copies.append(
            remote(
                cards_out.at[to_src, half], cards_in.at[src, half],
                card_send.at[turn - 1], card_recv.at[turn - 1], (to_src, seq),
            )
        )
        new_copies.append(
            remote(
                news_out.at[to_src], news_in.at[src],
                new_send.at[turn - 1], new_recv.at[turn - 1], (to_src, seq),
            )
        )
        swap_copies.append(
            remote(
                cards_in.at[from_src, half], cards_in.at[from_src, half],
                swap_send.at[turn - 1], swap_recv.at[turn - 1], sibling,
            )
        )
    for copy in card_copies:
        copy.start()

    @pl.when(seq == 0)
    def _():
        for copy in new_copies:
            copy.start()

    pump(WINDOW - PUMP_FIRST)
    for copy, swap in zip(card_copies, swap_copies):
        copy.wait_recv()
        swap.start()
    for copy, swap in zip(card_copies, swap_copies):
        copy.wait_send()
        swap.wait()

    @pl.when(seq == 0)
    def _():
        for copy in new_copies:
            copy.wait()

    late[2].wait()
    first = seq == 0
    ahead = lax.broadcasted_iota(jnp.int32, (1, SPAN), 1)
    in_position = ahead // GROUP * SPAN + seq * GROUP + ahead % GROUP
    res_position = seq * RES_SPAN + lax.broadcasted_iota(jnp.int32, (1, RES_SPAN), 1)
    row_id = lax.broadcasted_iota(jnp.int32, (ROWS, HEAD_SIZE), 0)
    lane_id = lax.broadcasted_iota(jnp.int32, (ROWS, HEAD_SIZE), 1)
    for block in range(4):
        in_live = in_position < lengths[block]
        res_live = res_position < res_len[src * 4 + block]
        for start in (0, 4):

            @pl.loop(start, start + 4, unroll=2)
            def _(head):
                keys = pl.ds(pl.multiple_of(head * HEAD_SIZE, HEAD_SIZE), HEAD_SIZE)
                values = pl.ds(pl.multiple_of(KEY_WIDTH + head * HEAD_SIZE, HEAD_SIZE), HEAD_SIZE)
                in_peak, in_total, in_sum = partial_of(
                    cards_in.at[block], news_in.at[block], rebuilt[block, :, keys], rebuilt[block, :, values],
                    in_live, first, head,
                )
                res_peak, res_total, res_sum = partial_of(
                    cards.at[4 + block], news.at[4 + block], resident[block, :, keys], resident[block, :, values],
                    res_live, first, head,
                )
                to_core, to_plane = head % 2, block * 4 + head // 2
                part_out[to_core, to_plane, 0] = in_sum.astype(jnp.bfloat16)
                part_out[to_core, to_plane, 1] = res_sum.astype(jnp.bfloat16)
                held = jnp.where(
                    lane_id < 64,
                    jnp.where(lane_id < 32, in_peak, in_total),
                    jnp.where(lane_id < 96, res_peak, res_total),
                )
                stat_out[to_core, to_plane] = jnp.sum(
                    jnp.where(lane_id % ROWS == row_id, held, 0.0), axis=0, keepdims=True
                )

            pump(PUMP_BLOCK)

    core_copies = [
        remote(
            stat_out.at[1 - core], core_stat, core_send.at[0], core_recv.at[0], sibling
        ),
        remote(
            part_out.at[1 - core], core_part, core_send.at[1], core_recv.at[1], sibling
        ),
    ]
    for copy in core_copies:
        copy.start()
    pump(PUMP_CORE)
    for copy in core_copies:
        copy.wait()

    def columns_of(row):
        return [
            jnp.sum(jnp.where(lane_id == row_id + lane, row, 0.0), axis=1, keepdims=True)
            for lane in (0, 64)
        ]

    stat_lane = lax.broadcasted_iota(jnp.int32, (1, HEAD_SIZE), 1)
    is_peak = stat_lane % 64 < 32

    @pl.loop(0, PLANE, unroll=4)
    def _(pair):
        here, there = stat_out[core, pair], core_stat[pair]
        peak = jnp.maximum(here, there)
        here_factor, there_factor = jnp.exp(here - peak), jnp.exp(there - peak)
        total = here * pltpu.roll(here_factor, ROWS, 1) + there * pltpu.roll(there_factor, ROWS, 1)
        joint_stat[pair] = jnp.where(is_peak, peak, total)
        here_columns, there_columns = columns_of(here_factor), columns_of(there_factor)
        for kind in range(2):
            joint_part[pair, kind] = (
                here_columns[kind] * part_out[core, pair, kind].astype(jnp.float32)
                + there_columns[kind] * core_part[pair, kind].astype(jnp.float32)
            ).astype(jnp.bfloat16)

    part_in[plane] = joint_part[plane]
    stat_in[plane] = joint_stat[plane]
    for offset in PLANE_OFFSETS:
        place = place_at(own, offset)
        to_plane = place[1] // 2
        remote(
            joint_stat.at[to_plane], stat_in.at[plane], pair_send.at[0], pair_recv.at[0], place
        ).start()
        remote(
            joint_part.at[to_plane], part_in.at[plane], pair_send.at[1], pair_recv.at[1], place
        ).start()
    pump(PUMP_PAIR)
    others = pl.ds(0, PLANE - 1)
    take_bytes(stat_in.at[others], pair_recv.at[0])
    take_bytes(part_in.at[others], pair_recv.at[1])
    stats = jnp.concatenate([stat_in[device] for device in range(PLANE)], axis=0)
    factor = jnp.exp(stats - jnp.max(stats, axis=0, keepdims=True))
    totals = pltpu.roll(stats, HEAD_SIZE - ROWS, 1)
    factors[...] = factor / jnp.sum(factor * totals, axis=0, keepdims=True)

    def add(device, sums):
        columns = columns_of(factors[pl.ds(device, 1), :])
        return tuple(
            sums[kind] + columns[kind] * part_in[device, kind].astype(jnp.float32)
            for kind in range(2)
        )

    zero = jnp.zeros((ROWS, HEAD_SIZE), jnp.float32)
    sums = lax.fori_loop(0, PLANE, add, (zero, zero), unroll=4)
    for kind in range(2):
        result[kind] = sums[kind].astype(jnp.bfloat16)

    row = src * 4 + z
    at_home = pltpu.make_async_copy(result.at[1], result_out.at[1, core, plane], own_sem)

    @pl.when(x == src)
    def _():
        pltpu.make_async_copy(result.at[0], result_out.at[0, core, row], result_recv.at[0]).start()
        pltpu.make_async_copy(result.at[0], unused, result_send.at[0]).start()

    @pl.when(x != src)
    def _():
        remote(
            result.at[0], result_out.at[0, core, row], result_send.at[0], result_recv.at[0],
            (x, seq),
        ).start()

    for offset in PLANE_OFFSETS:
        to_seq = place_at(own, offset)[1]
        remote(
            result.at[0], result_out.at[0, core, row], result_send.at[0], result_recv.at[0],
            (x, to_seq),
        ).start()
        remote(
            result.at[1], result_out.at[1, core, plane], result_send.at[1], result_recv.at[1],
            (src, to_seq),
        ).start()
    keep.wait()
    at_home.start()
    pump(len(work))
    for copy in copies[-WINDOW:]:
        copy.wait_send()
    at_home.wait()
    take_bytes(result_out.at[0, core], result_recv.at[0])
    take_bytes(result_out.at[1, core, others], result_recv.at[1])
    back_copies = [
        remote(
            result_out.at[kind, core], result_out.at[kind, core],
            back_send.at[kind], back_recv.at[kind], sibling,
        )
        for kind in range(2)
    ]
    for copy in back_copies:
        copy.start()
    take_bytes(stat_in.at[others], pair_send.at[0])
    take_bytes(part_in.at[others], pair_send.at[1])
    take_bytes(result_out.at[0, core], result_send.at[0])
    take_bytes(result_out.at[1, core, others], result_send.at[1])
    for copy in back_copies:
        copy.wait()
    take_bytes(recv_hbm.at[pl.ds(0, len(OFFSETS))], recv_sem)


def move(assign, in_len, res_len, delta, anchors, scales, resident, queries, fresh):
    any_space = pl.BlockSpec(memory_space=pl.ANY)
    bf16, f32 = jnp.bfloat16, jnp.float32
    operands = [
        pltpu.with_memory_space_constraint(a, pltpu.HBM)
        for a in (assign, in_len, res_len, delta, anchors, scales, resident, queries, fresh)
    ]
    return pl.pallas_call(
        move_kernel,
        out_shape=(
            pltpu.VMEM((N_SRC * N_SEQ, GROUP, FEAT), bf16),
            pltpu.VMEM((2, 2, PLANE, ROWS, HEAD_SIZE), bf16),
        ),
        in_specs=[pl.BlockSpec(memory_space=pltpu.HBM)] * 9,
        out_specs=(any_space, any_space),
        scratch_shapes=[
            pltpu.SMEM((16,), jnp.int32),
            pltpu.SMEM((16,), jnp.int32),
            pltpu.SMEM((16,), jnp.int32),
            pltpu.VMEM(delta.shape, bf16),
            pltpu.VMEM(anchors.shape, bf16),
            pltpu.VMEM(scales.shape, f32),
            pltpu.VMEM(resident.shape, bf16),
            pltpu.VMEM(queries.shape, bf16),
            pltpu.VMEM(fresh.shape, bf16),
            pltpu.VMEM((8, QUERY_ROWS, HEAD_SIZE), bf16),
            pltpu.VMEM((8, NEW_ROWS, HEAD_SIZE), bf16),
            pltpu.VMEM((N_SEQ, FEAT), f32),
            pltpu.VMEM((N_SEQ, FEAT), f32),
            pltpu.VMEM((N_SRC, SPAN, FEAT), bf16),
            pltpu.VMEM((N_SRC, QUERY_ROWS, HEAD_SIZE), bf16),
            pltpu.VMEM((N_SRC, QUERY_ROWS, HEAD_SIZE), bf16),
            pltpu.VMEM((N_SRC, NEW_ROWS, HEAD_SIZE), bf16),
            pltpu.VMEM((N_SRC, NEW_ROWS, HEAD_SIZE), bf16),
            pltpu.VMEM((2, PLANE, 2, ROWS, HEAD_SIZE), bf16),
            pltpu.VMEM((2, PLANE, 1, HEAD_SIZE), f32),
            pltpu.VMEM((PLANE, 2, ROWS, HEAD_SIZE), bf16),
            pltpu.VMEM((PLANE, 1, HEAD_SIZE), f32),
            pltpu.VMEM((PLANE, 2, ROWS, HEAD_SIZE), bf16),
            pltpu.VMEM((PLANE, 1, HEAD_SIZE), f32),
            pltpu.VMEM((PLANE, 2, ROWS, HEAD_SIZE), bf16),
            pltpu.VMEM((PLANE, 1, HEAD_SIZE), f32),
            pltpu.VMEM((PLANE, HEAD_SIZE), f32),
            pltpu.VMEM((2, ROWS, HEAD_SIZE), bf16),
            pltpu.VMEM((ROWS, HEAD_SIZE), bf16),
            pltpu.SemaphoreType.DMA((9,)),
            pltpu.SemaphoreType.DMA,
            pltpu.SemaphoreType.DMA((WINDOW,)),
            pltpu.SemaphoreType.DMA,
            pltpu.SemaphoreType.DMA((3,)),
            pltpu.SemaphoreType.DMA((3,)),
            pltpu.SemaphoreType.DMA((3,)),
            pltpu.SemaphoreType.DMA((3,)),
            pltpu.SemaphoreType.DMA((3,)),
            pltpu.SemaphoreType.DMA((3,)),
            pltpu.SemaphoreType.DMA((2,)),
            pltpu.SemaphoreType.DMA((2,)),
            pltpu.SemaphoreType.DMA((2,)),
            pltpu.SemaphoreType.DMA((2,)),
            pltpu.SemaphoreType.DMA((2,)),
            pltpu.SemaphoreType.DMA((2,)),
            pltpu.SemaphoreType.DMA((2,)),
            pltpu.SemaphoreType.DMA((2,)),
        ],
        compiler_params=pltpu.CompilerParams(
            collective_id=1, has_side_effects=True, vmem_limit_bytes=32 * MIB
        ),
    )(*operands)


EDGE = 64


def place_kernel(
    assign_hbm, in_len_hbm, recv, result_ref, in_cache, attention,
    assign, in_len, result, unpacked, zeros, edge, out_sem, edge_sem, load_sem,
):
    src, seq = lax.axis_index("src"), lax.axis_index("seq")
    loads = [
        pltpu.make_async_copy(assign_hbm, assign, load_sem.at[0]),
        pltpu.make_async_copy(in_len_hbm, in_len, load_sem.at[1]),
        pltpu.make_async_copy(result_ref, result, load_sem.at[2]),
    ]
    for load in loads:
        load.start()
    zeros[...] = jnp.zeros_like(zeros)
    for load in loads[:2]:
        load.wait()
    sources, counts = [], []
    for slot in range(4):
        source, length = jnp.int32(0), jnp.int32(0)
        for request in range(16):
            here = assign[request] == src * 4 + slot
            source = jnp.where(here, request // 4, source)
            length = jnp.where(here, in_len[request], length)
        count = jnp.clip(length - seq * SPAN, 0, SPAN)
        sources.append(source)
        counts.append(count)
        whole = count // EDGE
        cut = whole * EDGE < count

        @pl.when(whole == SPAN // EDGE)
        def _():
            pltpu.make_async_copy(recv.at[source], in_cache.at[slot], out_sem).start()

        @pl.when(whole < SPAN // EDGE)
        def _():
            for part in range(SPAN // EDGE):
                rows = pl.ds(part * EDGE, EDGE)

                @pl.when(part < whole)
                def _():
                    pltpu.make_async_copy(
                        recv.at[source, rows], in_cache.at[slot, rows], out_sem
                    ).start()

                @pl.when(jnp.logical_and(part == whole, cut))
                def _():
                    pltpu.make_async_copy(
                        recv.at[source, rows], edge.at[slot], edge_sem.at[slot]
                    ).start()

                @pl.when(jnp.logical_and(part >= whole, jnp.logical_or(part > whole, ~cut)))
                def _():
                    pltpu.make_async_copy(zeros, in_cache.at[slot, rows], out_sem).start()

    row = lax.broadcasted_iota(jnp.int32, (EDGE, FEAT), 0)
    for slot in range(4):
        whole = counts[slot] // EDGE

        @pl.when(whole * EDGE < counts[slot])
        def _():
            pltpu.make_async_copy(edge.at[slot], edge.at[slot], edge_sem.at[slot]).wait()
            kept = edge[slot]
            edge[slot] = jnp.where(row < counts[slot] - whole * EDGE, kept, jnp.zeros_like(kept))
            rows = pl.ds(pl.multiple_of(whole * EDGE, EDGE), EDGE)
            pltpu.make_async_copy(edge.at[slot], in_cache.at[slot, rows], out_sem).start()

    loads[2].wait()
    for slot in range(8):
        for head in range(KEY_VALUE_HEADS):
            first = sources[slot] if slot < 4 else slot - 4
            rows = result[slot // 4, head % 2, first * 4 + head // 2].astype(jnp.float32)
            for column in range(8):
                low = (head * 8 + column) * HEAD_SIZE
                unpacked[slot, :, low : low + HEAD_SIZE] = rows[
                    column * 4 : column * 4 + 4, :
                ].astype(jnp.bfloat16)
    last = pltpu.make_async_copy(unpacked, attention, load_sem.at[3])
    last.start()
    last.wait()
    pltpu.make_async_copy(in_cache, in_cache, out_sem).wait()


def place(assign, in_len, recv, result):
    any_space = pl.BlockSpec(memory_space=pl.ANY)
    attention = (8, 4, QUERY_HEADS * HEAD_SIZE)
    return pl.pallas_call(
        place_kernel,
        out_shape=(
            pltpu.HBM((4, SPAN, FEAT), jnp.bfloat16),
            pltpu.HBM(attention, jnp.bfloat16),
        ),
        in_specs=[any_space] * 4,
        out_specs=(any_space, any_space),
        scratch_shapes=[
            pltpu.SMEM((16,), jnp.int32),
            pltpu.SMEM((16,), jnp.int32),
            pltpu.VMEM(result.shape, jnp.bfloat16),
            pltpu.VMEM(attention, jnp.bfloat16),
            pltpu.VMEM((EDGE, FEAT), jnp.bfloat16),
            pltpu.VMEM((4, EDGE, FEAT), jnp.bfloat16),
            pltpu.SemaphoreType.DMA,
            pltpu.SemaphoreType.DMA((4,)),
            pltpu.SemaphoreType.DMA((4,)),
        ],
        compiler_params=pltpu.CompilerParams(vmem_limit_bytes=16 * MIB),
    )(
        pltpu.with_memory_space_constraint(assign, pltpu.HBM),
        pltpu.with_memory_space_constraint(in_len, pltpu.HBM),
        recv,
        result,
    )


def on_device(
    kv_delta, anchors, scales, in_len, assign, res_cache, res_len, queries, fresh_key_value
):
    recv, result = move(
        assign,
        in_len,
        res_len,
        kv_delta.reshape(4, N_SEQ, GROUP, FEAT),
        anchors.reshape(4, N_SEQ, FEAT),
        scales.reshape(4, N_SEQ, FEAT // HEAD_SIZE).transpose(0, 2, 1),
        res_cache,
        queries,
        fresh_key_value,
    )
    return place(assign, in_len, recv.reshape(4, SPAN, FEAT), result)


def solution(mesh):
    in_specs = (
        P("src", None, "seq", None, None),
        P("src", None, "seq", None),
        P("src", None, "seq", None),
        P(),
        P(),
        P("src", "seq", None),
        P(),
        P("src", None, None),
        P("src", None, None),
    )
    out_specs = (P("src", "seq", None), P("src", None, None))
    return jax.shard_map(
        on_device, mesh=mesh, in_specs=in_specs, out_specs=out_specs, check_vma=False
    )
```

```python
import functools
import itertools
import math

import jax
import jax.numpy as jnp
from jax import lax
from jax.experimental import pallas as pl
from jax.experimental.pallas import tpu as pltpu
from jax.sharding import PartitionSpec as P

QUERY_HEADS = 64
KEY_VALUE_HEADS = 8
HEAD_SIZE = 128
GROUP = 16
N_SRC = 4
N_SEQ = 32
FEAT = 2048
KEY_WIDTH = KEY_VALUE_HEADS * HEAD_SIZE
MESH = pl.DeviceIdType.MESH
MIB = 2**20


def orbit(offset):
    y, x, z, core = offset
    found = []
    for sign in (1, -1):
        for turned in ((y, x, z), (z, y, x), (x, z, y)):
            found.append(tuple((sign * v) % 4 for v in turned) + (core,))
    return found


def send_offsets():
    every = [o for o in itertools.product(range(4), range(4), range(4), range(2)) if any(o)]
    hops = lambda o: sum(min(v, 4 - v) for v in o[:3])
    ordered = []
    for offset in sorted(every, key=lambda o: -hops(o)):
        for turned in orbit(offset):
            if turned not in ordered:
                ordered.append(turned)
    mixed = []
    for near in range(64):
        mixed.append(ordered[near])
        mixed.append(ordered[126 - near])
    return list(dict.fromkeys(mixed))


OFFSETS = send_offsets()


def own_place():
    src = lax.axis_index("src")
    seq = lax.axis_index("seq")
    return src, seq // 8, lax.rem(seq // 2, 4), lax.rem(seq, 2)


def place_at(own, offset):
    src, x, z, core = own
    dy, dx, dz, dcore = offset
    to_src = lax.rem(src + dy, 4) if dy else src
    to_x = lax.rem(x + dx, 4) if dx else x
    to_z = lax.rem(z + dz, 4) if dz else z
    to_core = 1 - core if dcore else core
    return to_src, to_x * 8 + to_z * 2 + to_core

SPAN = N_SEQ * GROUP
RES_SPAN = 256
ROWS = 32
QUERY_ROWS = KEY_VALUE_HEADS * ROWS
NEW_ROWS = KEY_VALUE_HEADS * GROUP
LOWEST = -1e30
WINDOW = 170
PUMP_FIRST, PUMP_BLOCK, PUMP_CORE, PUMP_PAIR = 40, 8, 6, 8
PLANE_OFFSETS = [o for o in OFFSETS if o[0] == 0 and o[3] == 0]
PLANE = 16


def remote(src_ref, dst_ref, send_sem, recv_sem, place):
    return pltpu.make_async_remote_copy(
        src_ref=src_ref,
        dst_ref=dst_ref,
        send_sem=send_sem,
        recv_sem=recv_sem,
        device_id=place,
        device_id_type=MESH,
    )


def take_bytes(ref, sem):
    pltpu.make_async_copy(ref, ref, sem).wait()


def partial_of(card, news, cache_keys, cache_values, live, first, head):
    query = card[pl.ds(pl.multiple_of(head * ROWS, ROWS), ROWS), :]
    fresh = news[pl.ds(pl.multiple_of(head * GROUP, GROUP), GROUP), :]
    fresh = jnp.where(first, fresh, jnp.zeros_like(fresh))
    across = (((1,), (1,)), ((), ()))
    unit = 1.0 / math.sqrt(HEAD_SIZE)
    scores = lax.dot_general(query, cache_keys, across, preferred_element_type=jnp.float32) * unit
    new_scores = lax.dot_general(query, fresh, across, preferred_element_type=jnp.float32) * unit
    step = lax.broadcasted_iota(jnp.int32, (ROWS, GROUP), 0) % 4
    token = lax.broadcasted_iota(jnp.int32, (ROWS, GROUP), 1)
    new_live = jnp.logical_and(token <= step, first)
    scores = jnp.where(live, scores, LOWEST)
    new_scores = jnp.where(new_live, new_scores, LOWEST)
    peak = jnp.maximum(
        jnp.max(scores, axis=1, keepdims=True), jnp.max(new_scores, axis=1, keepdims=True)
    )
    weights = jnp.where(live, jnp.exp(scores - peak), 0.0)
    new_weights = jnp.where(new_live, jnp.exp(new_scores - peak), 0.0)
    total = jnp.sum(weights, axis=1, keepdims=True) + jnp.sum(new_weights, axis=1, keepdims=True)
    summed = jnp.dot(
        weights.astype(jnp.bfloat16), cache_values, preferred_element_type=jnp.float32
    )
    rounded = new_weights.astype(jnp.bfloat16).astype(jnp.float32)
    fresh = fresh.astype(jnp.float32)
    for new in range(4):
        summed = summed + rounded[:, new : new + 1] * fresh[4 + new : 5 + new, :]
    return peak, total, summed


def read_cards(queries, fresh, cards, news):
    @pl.loop(0, 8)
    def _(slot):
        asked = queries[slot].astype(jnp.float32)
        new = fresh[slot].astype(jnp.float32)
        for head in range(KEY_VALUE_HEADS):
            rows = [
                asked[:, column * HEAD_SIZE : (column + 1) * HEAD_SIZE]
                for column in range(head * 8, head * 8 + 8)
            ]
            cards[slot, head * ROWS : (head + 1) * ROWS, :] = jnp.concatenate(
                rows, axis=0
            ).astype(jnp.bfloat16)
            low = head * HEAD_SIZE
            rows = [
                new[:, low : low + HEAD_SIZE],
                new[:, KEY_WIDTH + low : KEY_WIDTH + low + HEAD_SIZE],
                jnp.zeros((8, HEAD_SIZE), jnp.float32),
            ]
            news[slot, head * GROUP : (head + 1) * GROUP, :] = jnp.concatenate(
                rows, axis=0
            ).astype(jnp.bfloat16)


def move_kernel(
    assign_hbm, in_len_hbm, res_len_hbm, delta_hbm, anchors_hbm, scales_hbm, resident_hbm, queries_hbm,
    fresh_hbm, recv_hbm, result_out,
    assign, in_len, res_len, delta, anchors, scales, resident, queries, fresh, cards, news, anchor_rows, scale_rows, rebuilt,
    cards_out, cards_in, news_out, news_in, part_out, stat_out, core_part, core_stat, joint_part, joint_stat,
    part_in, stat_in, factors, result, unused,
    load_sem, own_sem, send_sem, recv_sem, card_send, card_recv, new_send, new_recv, swap_send, swap_recv, core_send, core_recv,
    pair_send, pair_recv, result_send, result_recv, back_send, back_recv,
):
    own = own_place()
    src, seq = lax.axis_index("src"), lax.axis_index("seq")
    x, z, core = own[1:]
    plane = x * 4 + z
    sibling = (src, seq + 1 - 2 * core)
    loads = [
        pltpu.make_async_copy(anchors_hbm, anchors, load_sem.at[0]),
        pltpu.make_async_copy(scales_hbm, scales, load_sem.at[1]),
        pltpu.make_async_copy(delta_hbm, delta, load_sem.at[2]),
        pltpu.make_async_copy(queries_hbm, queries, load_sem.at[3]),
        pltpu.make_async_copy(fresh_hbm, fresh, load_sem.at[4]),
        pltpu.make_async_copy(resident_hbm, resident, load_sem.at[5]),
        pltpu.make_async_copy(assign_hbm, assign, load_sem.at[6]),
        pltpu.make_async_copy(in_len_hbm, in_len, load_sem.at[7]),
        pltpu.make_async_copy(res_len_hbm, res_len, load_sem.at[8]),
    ]
    early, late = loads[:3] + loads[6:], loads[3:6]
    loads[2].start()
    barrier = pltpu.get_barrier_semaphore()
    for offset in OFFSETS:
        pl.semaphore_signal(barrier, inc=1, device_id=place_at(own, offset), device_id_type=MESH)
    for load in loads[:2] + loads[6:] + late:
        load.start()
    for load in early:
        load.wait()
    same_group = lax.broadcasted_iota(jnp.int32, (N_SEQ, N_SEQ), 0) == lax.broadcasted_iota(
        jnp.int32, (N_SEQ, N_SEQ), 1
    )
    lengths = []
    for target in range(N_SRC):
        request, length = jnp.int32(0), jnp.int32(0)
        for local in range(4):
            slot = assign[src * 4 + local]
            here = jnp.logical_and(slot >= target * 4, slot < target * 4 + 4)
            request = jnp.where(here, local, request)
            length = jnp.where(here, in_len[src * 4 + local], length)
        lengths.append(length)
        anchor_rows[...] = anchors[request].astype(jnp.float32)
        scale = scales[request]
        for head in range(FEAT // HEAD_SIZE):
            column = jnp.sum(
                jnp.where(same_group, scale[head : head + 1, :], 0.0), axis=1, keepdims=True
            )
            scale_rows[:, head * HEAD_SIZE : (head + 1) * HEAD_SIZE] = jnp.broadcast_to(
                column, (N_SEQ, HEAD_SIZE)
            )

        @pl.loop(0, N_SEQ, unroll=2)
        def _(group):
            rows = anchor_rows[pl.ds(group, 1), :] + scale_rows[pl.ds(group, 1), :] * delta[
                request, group
            ].reshape(GROUP, FEAT).astype(jnp.float32)
            rebuilt[target, pl.ds(pl.multiple_of(group * GROUP, GROUP), GROUP), :] = rows.astype(
                jnp.bfloat16
            )

    mine = src * N_SEQ + seq
    keep = pltpu.make_async_copy(
        rebuilt.at[src, pl.ds(pl.multiple_of(seq * GROUP, GROUP), GROUP), :],
        recv_hbm.at[mine],
        own_sem,
    )
    keep.start()
    pl.semaphore_wait(barrier, len(OFFSETS))

    copies = []
    work = [(half, offset) for half in range(2) for offset in OFFSETS]

    def pump(count):
        for half, offset in work[len(copies) : len(copies) + count]:
            to_src, to_seq = place_at(own, offset)
            columns = pl.ds(half * (FEAT // 2), FEAT // 2)
            number = len(copies)
            if number >= WINDOW:
                copies[number - WINDOW].wait_send()
            copy = remote(
                rebuilt.at[to_src, pl.ds(pl.multiple_of(to_seq * GROUP, GROUP), GROUP), columns],
                recv_hbm.at[mine, :, columns],
                send_sem.at[number % WINDOW],
                recv_sem,
                (to_src, to_seq),
            )
            copy.start()
            copies.append(copy)

    pump(PUMP_FIRST)
    for load in late[:2]:
        load.wait()
    read_cards(queries, fresh, cards, news)
    for source in range(N_SRC):
        place = jnp.int32(0)
        for local in range(4):
            slot = assign[source * 4 + local] - src * 4
            place = jnp.where(jnp.logical_and(slot >= 0, slot < 4), slot, place)
        cards_out[source] = cards[place]
        news_out[source] = news[place]
    cards_in[src] = cards_out[src]
    news_in[src] = news_out[src]
    half = pl.ds(pl.multiple_of(core * (QUERY_ROWS // 2), QUERY_ROWS // 2), QUERY_ROWS // 2)
    card_copies, new_copies, swap_copies = [], [], []
    for turn in range(1, N_SRC):
        to_src = lax.rem(src + turn, N_SRC)
        from_src = lax.rem(src + N_SRC - turn, N_SRC)
        card_copies.append(
            remote(
                cards_out.at[to_src, half], cards_in.at[src, half],
                card_send.at[turn - 1], card_recv.at[turn - 1], (to_src, seq),
            )
        )
        new_copies.append(
            remote(
                news_out.at[to_src], news_in.at[src],
                new_send.at[turn - 1], new_recv.at[turn - 1], (to_src, seq),
            )
        )
        swap_copies.append(
            remote(
                cards_in.at[from_src, half], cards_in.at[from_src, half],
                swap_send.at[turn - 1], swap_recv.at[turn - 1], sibling,
            )
        )
    for copy in card_copies:
        copy.start()

    @pl.when(seq == 0)
    def _():
        for copy in new_copies:
            copy.start()

    pump(WINDOW - PUMP_FIRST)
    for copy, swap in zip(card_copies, swap_copies):
        copy.wait_recv()
        swap.start()
    for copy, swap in zip(card_copies, swap_copies):
        copy.wait_send()
        swap.wait()

    @pl.when(seq == 0)
    def _():
        for copy in new_copies:
            copy.wait()

    late[2].wait()
    first = seq == 0
    ahead = lax.broadcasted_iota(jnp.int32, (1, SPAN), 1)
    in_position = ahead // GROUP * SPAN + seq * GROUP + ahead % GROUP
    res_position = seq * RES_SPAN + lax.broadcasted_iota(jnp.int32, (1, RES_SPAN), 1)
    row_id = lax.broadcasted_iota(jnp.int32, (ROWS, HEAD_SIZE), 0)
    lane_id = lax.broadcasted_iota(jnp.int32, (ROWS, HEAD_SIZE), 1)
    for block in range(4):
        in_live = in_position < lengths[block]
        res_live = res_position < res_len[src * 4 + block]
        for start in (0, 4):

            @pl.loop(start, start + 4, unroll=2)
            def _(head):
                keys = pl.ds(pl.multiple_of(head * HEAD_SIZE, HEAD_SIZE), HEAD_SIZE)
                values = pl.ds(pl.multiple_of(KEY_WIDTH + head * HEAD_SIZE, HEAD_SIZE), HEAD_SIZE)
                in_peak, in_total, in_sum = partial_of(
                    cards_in.at[block], news_in.at[block], rebuilt[block, :, keys], rebuilt[block, :, values],
                    in_live, first, head,
                )
                res_peak, res_total, res_sum = partial_of(
                    cards.at[4 + block], news.at[4 + block], resident[block, :, keys], resident[block, :, values],
                    res_live, first, head,
                )
                to_core, to_plane = head % 2, block * 4 + head // 2
                part_out[to_core, to_plane, 0] = in_sum.astype(jnp.bfloat16)
                part_out[to_core, to_plane, 1] = res_sum.astype(jnp.bfloat16)
                held = jnp.where(
                    lane_id < 64,
                    jnp.where(lane_id < 32, in_peak, in_total),
                    jnp.where(lane_id < 96, res_peak, res_total),
                )
                stat_out[to_core, to_plane] = jnp.sum(
                    jnp.where(lane_id % ROWS == row_id, held, 0.0), axis=0, keepdims=True
                )

            pump(PUMP_BLOCK)

    core_copies = [
        remote(
            stat_out.at[1 - core], core_stat, core_send.at[0], core_recv.at[0], sibling
        ),
        remote(
            part_out.at[1 - core], core_part, core_send.at[1], core_recv.at[1], sibling
        ),
    ]
    for copy in core_copies:
        copy.start()
    pump(PUMP_CORE)
    for copy in core_copies:
        copy.wait()

    def columns_of(row):
        return [
            jnp.sum(jnp.where(lane_id == row_id + lane, row, 0.0), axis=1, keepdims=True)
            for lane in (0, 64)
        ]

    stat_lane = lax.broadcasted_iota(jnp.int32, (1, HEAD_SIZE), 1)
    is_peak = stat_lane % 64 < 32

    @pl.loop(0, PLANE, unroll=4)
    def _(pair):
        here, there = stat_out[core, pair], core_stat[pair]
        peak = jnp.maximum(here, there)
        here_factor, there_factor = jnp.exp(here - peak), jnp.exp(there - peak)
        total = here * pltpu.roll(here_factor, ROWS, 1) + there * pltpu.roll(there_factor, ROWS, 1)
        joint_stat[pair] = jnp.where(is_peak, peak, total)
        here_columns, there_columns = columns_of(here_factor), columns_of(there_factor)
        for kind in range(2):
            joint_part[pair, kind] = (
                here_columns[kind] * part_out[core, pair, kind].astype(jnp.float32)
                + there_columns[kind] * core_part[pair, kind].astype(jnp.float32)
            ).astype(jnp.bfloat16)

    part_in[plane] = joint_part[plane]
    stat_in[plane] = joint_stat[plane]
    for offset in PLANE_OFFSETS:
        place = place_at(own, offset)
        to_plane = place[1] // 2
        remote(
            joint_stat.at[to_plane], stat_in.at[plane], pair_send.at[0], pair_recv.at[0], place
        ).start()
        remote(
            joint_part.at[to_plane], part_in.at[plane], pair_send.at[1], pair_recv.at[1], place
        ).start()
    pump(PUMP_PAIR)
    others = pl.ds(0, PLANE - 1)
    take_bytes(stat_in.at[others], pair_recv.at[0])
    take_bytes(part_in.at[others], pair_recv.at[1])
    stats = jnp.concatenate([stat_in[device] for device in range(PLANE)], axis=0)
    factor = jnp.exp(stats - jnp.max(stats, axis=0, keepdims=True))
    totals = pltpu.roll(stats, HEAD_SIZE - ROWS, 1)
    factors[...] = factor / jnp.sum(factor * totals, axis=0, keepdims=True)

    def add(device, sums):
        columns = columns_of(factors[pl.ds(device, 1), :])
        return tuple(
            sums[kind] + columns[kind] * part_in[device, kind].astype(jnp.float32)
            for kind in range(2)
        )

    zero = jnp.zeros((ROWS, HEAD_SIZE), jnp.float32)
    sums = lax.fori_loop(0, PLANE, add, (zero, zero), unroll=4)
    for kind in range(2):
        result[kind] = sums[kind].astype(jnp.bfloat16)

    row = src * 4 + z
    at_home = pltpu.make_async_copy(result.at[1], result_out.at[1, core, plane], own_sem)

    @pl.when(x == src)
    def _():
        pltpu.make_async_copy(result.at[0], result_out.at[0, core, row], result_recv.at[0]).start()
        pltpu.make_async_copy(result.at[0], unused, result_send.at[0]).start()

    @pl.when(x != src)
    def _():
        remote(
            result.at[0], result_out.at[0, core, row], result_send.at[0], result_recv.at[0],
            (x, seq),
        ).start()

    for offset in PLANE_OFFSETS:
        to_seq = place_at(own, offset)[1]
        remote(
            result.at[0], result_out.at[0, core, row], result_send.at[0], result_recv.at[0],
            (x, to_seq),
        ).start()
        remote(
            result.at[1], result_out.at[1, core, plane], result_send.at[1], result_recv.at[1],
            (src, to_seq),
        ).start()
    keep.wait()
    at_home.start()
    pump(len(work))
    for copy in copies[-WINDOW:]:
        copy.wait_send()
    at_home.wait()
    take_bytes(result_out.at[0, core], result_recv.at[0])
    take_bytes(result_out.at[1, core, others], result_recv.at[1])
    back_copies = [
        remote(
            result_out.at[kind, core], result_out.at[kind, core],
            back_send.at[kind], back_recv.at[kind], sibling,
        )
        for kind in range(2)
    ]
    for copy in back_copies:
        copy.start()
    take_bytes(stat_in.at[others], pair_send.at[0])
    take_bytes(part_in.at[others], pair_send.at[1])
    take_bytes(result_out.at[0, core], result_send.at[0])
    take_bytes(result_out.at[1, core, others], result_send.at[1])
    for copy in back_copies:
        copy.wait()
    take_bytes(recv_hbm.at[pl.ds(0, len(OFFSETS))], recv_sem)


def move(assign, in_len, res_len, delta, anchors, scales, resident, queries, fresh):
    any_space = pl.BlockSpec(memory_space=pl.ANY)
    bf16, f32 = jnp.bfloat16, jnp.float32
    operands = [
        pltpu.with_memory_space_constraint(a, pltpu.HBM)
        for a in (assign, in_len, res_len, delta, anchors, scales, resident, queries, fresh)
    ]
    return pl.pallas_call(
        move_kernel,
        out_shape=(
            pltpu.VMEM((N_SRC * N_SEQ, GROUP, FEAT), bf16),
            pltpu.VMEM((2, 2, PLANE, ROWS, HEAD_SIZE), bf16),
        ),
        in_specs=[pl.BlockSpec(memory_space=pltpu.HBM)] * 9,
        out_specs=(any_space, any_space),
        scratch_shapes=[
            pltpu.SMEM((16,), jnp.int32),
            pltpu.SMEM((16,), jnp.int32),
            pltpu.SMEM((16,), jnp.int32),
            pltpu.VMEM(delta.shape, bf16),
            pltpu.VMEM(anchors.shape, bf16),
            pltpu.VMEM(scales.shape, f32),
            pltpu.VMEM(resident.shape, bf16),
            pltpu.VMEM(queries.shape, bf16),
            pltpu.VMEM(fresh.shape, bf16),
            pltpu.VMEM((8, QUERY_ROWS, HEAD_SIZE), bf16),
            pltpu.VMEM((8, NEW_ROWS, HEAD_SIZE), bf16),
            pltpu.VMEM((N_SEQ, FEAT), f32),
            pltpu.VMEM((N_SEQ, FEAT), f32),
            pltpu.VMEM((N_SRC, SPAN, FEAT), bf16),
            pltpu.VMEM((N_SRC, QUERY_ROWS, HEAD_SIZE), bf16),
            pltpu.VMEM((N_SRC, QUERY_ROWS, HEAD_SIZE), bf16),
            pltpu.VMEM((N_SRC, NEW_ROWS, HEAD_SIZE), bf16),
            pltpu.VMEM((N_SRC, NEW_ROWS, HEAD_SIZE), bf16),
            pltpu.VMEM((2, PLANE, 2, ROWS, HEAD_SIZE), bf16),
            pltpu.VMEM((2, PLANE, 1, HEAD_SIZE), f32),
            pltpu.VMEM((PLANE, 2, ROWS, HEAD_SIZE), bf16),
            pltpu.VMEM((PLANE, 1, HEAD_SIZE), f32),
            pltpu.VMEM((PLANE, 2, ROWS, HEAD_SIZE), bf16),
            pltpu.VMEM((PLANE, 1, HEAD_SIZE), f32),
            pltpu.VMEM((PLANE, 2, ROWS, HEAD_SIZE), bf16),
            pltpu.VMEM((PLANE, 1, HEAD_SIZE), f32),
            pltpu.VMEM((PLANE, HEAD_SIZE), f32),
            pltpu.VMEM((2, ROWS, HEAD_SIZE), bf16),
            pltpu.VMEM((ROWS, HEAD_SIZE), bf16),
            pltpu.SemaphoreType.DMA((9,)),
            pltpu.SemaphoreType.DMA,
            pltpu.SemaphoreType.DMA((WINDOW,)),
            pltpu.SemaphoreType.DMA,
            pltpu.SemaphoreType.DMA((3,)),
            pltpu.SemaphoreType.DMA((3,)),
            pltpu.SemaphoreType.DMA((3,)),
            pltpu.SemaphoreType.DMA((3,)),
            pltpu.SemaphoreType.DMA((3,)),
            pltpu.SemaphoreType.DMA((3,)),
            pltpu.SemaphoreType.DMA((2,)),
            pltpu.SemaphoreType.DMA((2,)),
            pltpu.SemaphoreType.DMA((2,)),
            pltpu.SemaphoreType.DMA((2,)),
            pltpu.SemaphoreType.DMA((2,)),
            pltpu.SemaphoreType.DMA((2,)),
            pltpu.SemaphoreType.DMA((2,)),
            pltpu.SemaphoreType.DMA((2,)),
        ],
        compiler_params=pltpu.CompilerParams(
            collective_id=1, has_side_effects=True, vmem_limit_bytes=32 * MIB
        ),
    )(*operands)


EDGE = 64


def place_kernel(
    assign_hbm, in_len_hbm, recv, result_ref, in_cache, attention,
    assign, in_len, result, unpacked, zeros, edge, out_sem, edge_sem, load_sem,
):
    src, seq = lax.axis_index("src"), lax.axis_index("seq")
    loads = [
        pltpu.make_async_copy(assign_hbm, assign, load_sem.at[0]),
        pltpu.make_async_copy(in_len_hbm, in_len, load_sem.at[1]),
        pltpu.make_async_copy(result_ref, result, load_sem.at[2]),
    ]
    for load in loads:
        load.start()
    zeros[...] = jnp.zeros_like(zeros)
    for load in loads[:2]:
        load.wait()
    sources, counts = [], []
    for slot in range(4):
        source, length = jnp.int32(0), jnp.int32(0)
        for request in range(16):
            here = assign[request] == src * 4 + slot
            source = jnp.where(here, request // 4, source)
            length = jnp.where(here, in_len[request], length)
        count = jnp.clip(length - seq * SPAN, 0, SPAN)
        sources.append(source)
        counts.append(count)
        whole = count // EDGE
        cut = whole * EDGE < count

        @pl.when(whole == SPAN // EDGE)
        def _():
            for part in range(4):
                rows = pl.ds(part * (SPAN // 4), SPAN // 4)
                pltpu.make_async_copy(
                    recv.at[source, rows], in_cache.at[slot, rows], out_sem
                ).start()

        @pl.when(whole < SPAN // EDGE)
        def _():
            for part in range(SPAN // EDGE):
                rows = pl.ds(part * EDGE, EDGE)

                @pl.when(part < whole)
                def _():
                    pltpu.make_async_copy(
                        recv.at[source, rows], in_cache.at[slot, rows], out_sem
                    ).start()

                @pl.when(jnp.logical_and(part == whole, cut))
                def _():
                    pltpu.make_async_copy(
                        recv.at[source, rows], edge.at[slot], edge_sem.at[slot]
                    ).start()

                @pl.when(jnp.logical_and(part >= whole, jnp.logical_or(part > whole, ~cut)))
                def _():
                    pltpu.make_async_copy(zeros, in_cache.at[slot, rows], out_sem).start()

    row = lax.broadcasted_iota(jnp.int32, (EDGE, FEAT), 0)
    for slot in range(4):
        whole = counts[slot] // EDGE

        @pl.when(whole * EDGE < counts[slot])
        def _():
            pltpu.make_async_copy(edge.at[slot], edge.at[slot], edge_sem.at[slot]).wait()
            kept = edge[slot]
            edge[slot] = jnp.where(row < counts[slot] - whole * EDGE, kept, jnp.zeros_like(kept))
            rows = pl.ds(pl.multiple_of(whole * EDGE, EDGE), EDGE)
            pltpu.make_async_copy(edge.at[slot], in_cache.at[slot, rows], out_sem).start()

    loads[2].wait()
    for slot in range(8):
        for head in range(KEY_VALUE_HEADS):
            first = sources[slot] if slot < 4 else slot - 4
            rows = result[slot // 4, head % 2, first * 4 + head // 2].astype(jnp.float32)
            for column in range(8):
                low = (head * 8 + column) * HEAD_SIZE
                unpacked[slot, :, low : low + HEAD_SIZE] = rows[
                    column * 4 : column * 4 + 4, :
                ].astype(jnp.bfloat16)
    last = pltpu.make_async_copy(unpacked, attention, load_sem.at[3])
    last.start()
    last.wait()
    pltpu.make_async_copy(in_cache, in_cache, out_sem).wait()


def place(assign, in_len, recv, result):
    any_space = pl.BlockSpec(memory_space=pl.ANY)
    attention = (8, 4, QUERY_HEADS * HEAD_SIZE)
    return pl.pallas_call(
        place_kernel,
        out_shape=(
            pltpu.HBM((4, SPAN, FEAT), jnp.bfloat16),
            pltpu.HBM(attention, jnp.bfloat16),
        ),
        in_specs=[any_space] * 4,
        out_specs=(any_space, any_space),
        scratch_shapes=[
            pltpu.SMEM((16,), jnp.int32),
            pltpu.SMEM((16,), jnp.int32),
            pltpu.VMEM(result.shape, jnp.bfloat16),
            pltpu.VMEM(attention, jnp.bfloat16),
            pltpu.VMEM((EDGE, FEAT), jnp.bfloat16),
            pltpu.VMEM((4, EDGE, FEAT), jnp.bfloat16),
            pltpu.SemaphoreType.DMA,
            pltpu.SemaphoreType.DMA((4,)),
            pltpu.SemaphoreType.DMA((4,)),
        ],
        compiler_params=pltpu.CompilerParams(vmem_limit_bytes=16 * MIB),
    )(
        pltpu.with_memory_space_constraint(assign, pltpu.HBM),
        pltpu.with_memory_space_constraint(in_len, pltpu.HBM),
        recv,
        result,
    )


def on_device(
    kv_delta, anchors, scales, in_len, assign, res_cache, res_len, queries, fresh_key_value
):
    recv, result = move(
        assign,
        in_len,
        res_len,
        kv_delta.reshape(4, N_SEQ, GROUP, FEAT),
        anchors.reshape(4, N_SEQ, FEAT),
        scales.reshape(4, N_SEQ, FEAT // HEAD_SIZE).transpose(0, 2, 1),
        res_cache,
        queries,
        fresh_key_value,
    )
    return place(assign, in_len, recv.reshape(4, SPAN, FEAT), result)


def solution(mesh):
    in_specs = (
        P("src", None, "seq", None, None),
        P("src", None, "seq", None),
        P("src", None, "seq", None),
        P(),
        P(),
        P("src", "seq", None),
        P(),
        P("src", None, None),
        P("src", None, None),
    )
    out_specs = (P("src", "seq", None), P("src", None, None))
    return jax.shard_map(
        on_device, mesh=mesh, in_specs=in_specs, out_specs=out_specs, check_vma=False
    )
```
